32 devices in a mesh: groups: 2 (over y), tm: 4 (over z), space: 2 (over x), clip: 2 (over core).
Axes of the slice: x: 2, y: 2, z: 4, core: 2. Of those that a mesh axis runs over, the one named last changes fastest.
Arguments:
- latents: bfloat16 [4, 16, 8, 6144], P(('groups', 'clip'), 'tm', 'space'), parts along dimension 0, may hold values from -6 to 6
- frame_counts: int32 [4], P(('groups', 'clip')), parts along dimension 0, may hold values from 2 to 16, as said below
- gain_first: float32 [192], replicated, may hold values from 0.5 to 1.5
- bias_first: float32 [192], replicated, may hold values from -3 to 3
- weight_first: bfloat16 [3, 3, 3, 192, 192], replicated, may hold values from -0.078125 to 0.078125
- gain_second: float32 [192], replicated, may hold values from 0.5 to 1.5
- bias_second: float32 [192], replicated, may hold values from -3 to 3
- weight_second: bfloat16 [3, 3, 3, 192, 192], replicated, may hold values from -0.078125 to 0.078125
Outputs:
- encoded: bfloat16 [4, 16, 8, 6144], P(('groups', 'clip'), 'tm', 'space'), parts along dimension 0
The draws below stay inside these ranges and needn't reach their ends.
There are 2 independent parts, one for each index of `groups`. The reference program is written for one: setup_inputs(seed, part) draws one part's arguments, and reference() takes and returns one part's arrays. A program takes and returns all parts, laid end to end along the dimension named above; an argument that names none is the same for every part. Nothing has to cross between parts.
Inputs may be any that keep to these rules, and one draw needn't show every extreme that they name: `frame_counts`: in every part exactly one clip has all 16 frames valid; every other clip has fewer.
All inputs are finite; a program needn't handle non-finite values.
Results may differ from the reference program's by a relative error of at most 0.007.
Values may be sent and summed in bfloat16 or wider, within the bound.
A program may use at most 64 MiB of HBM per device.

```python
import jax
import jax.numpy as jnp
from jax import lax

C = 192
COLS = 32
CLIPS = 2
FRAMES = 16
ROWS = 8


def draw_frame_counts(key, part):
    count_key = jax.random.fold_in(key, 11)
    pick_key = jax.random.fold_in(key, 23)
    drawn = jax.random.randint(count_key, (CLIPS,), 2, FRAMES)
    full_clip = jax.random.randint(pick_key, (), 0, CLIPS)
    return jnp.where(jnp.arange(CLIPS, dtype=jnp.int32) == full_clip, FRAMES, drawn).astype(jnp.int32)


def level_of(key, dims, shards, smallest, largest):
    level = 1.0
    for axis_at, blocks in shards:
        draws = jax.random.uniform(jax.random.fold_in(jax.random.fold_in(key, 6), axis_at), (blocks,), jnp.float32, smallest / len(shards), largest / len(shards))
        level = level * jnp.repeat(jnp.exp(draws), dims[axis_at] // blocks).reshape((-1,) + (1,) * (len(dims) - 1 - axis_at))
    return level


def noise(own_key, extent, deviation, most, pieces=(), kind=jnp.bfloat16):
    values = deviation * jax.random.normal(own_key, extent, jnp.float32)
    if pieces:
        values = values * level_of(own_key, extent, pieces, -0.22, 0.18)
    return jnp.clip(values, -most, most).astype(kind)


def setup_inputs(seed: int = 0, part: int = 0) -> dict:
    splits = jax.random.split(jax.random.key(seed), 9)
    part_splits = jax.random.split(jax.random.fold_in(splits[8], part), 9)
    latents = noise(part_splits[0], (CLIPS, FRAMES, ROWS, COLS * C), 1.0, 6.0, ((0, 2), (1, 4), (2, 2)))
    frame_counts = draw_frame_counts(jax.random.fold_in(jax.random.fold_in(splits[8], part), 71), part)
    gain_first = jnp.clip(jax.random.uniform(splits[2], (C,), jnp.float32, 0.5, 1.5), 0.5, 1.5)
    bias_first = noise(splits[3], (C,), 0.5, 3.0, (), jnp.float32)
    weight_first = noise(splits[4], (3, 3, 3, C, C), (27 * C) ** -0.5, 0.078125)
    gain_second = jnp.clip(jax.random.uniform(splits[5], (C,), jnp.float32, 0.5, 1.5), 0.5, 1.5)
    bias_second = noise(splits[6], (C,), 0.5, 3.0, (), jnp.float32)
    weight_second = noise(splits[7], (3, 3, 3, C, C), (27 * C) ** -0.5, 0.078125)
    return dict(latents=latents, frame_counts=frame_counts, gain_first=gain_first, bias_first=bias_first, weight_first=weight_first, gain_second=gain_second, bias_second=bias_second, weight_second=weight_second)


def norm_silu(values, gain):
    values = values.astype(jnp.float32)
    mean_square = lax.optimization_barrier(jnp.mean(values * values, axis=-1, keepdims=True))
    scaled = values * lax.rsqrt(mean_square + 1e-06) * gain
    return jax.nn.silu(scaled).astype(jnp.bfloat16)

def causal_conv(inputs, kernel):
    return lax.conv_general_dilated(inputs.astype(jnp.float32), kernel.astype(jnp.float32), (1, 1, 1), ((2, 0), (1, 1), (1, 1)), dimension_numbers=('NDHWC', 'DHWIO', 'NDHWC'), precision=lax.Precision.HIGHEST)

def reference(latents, frame_counts, gain_first, bias_first, weight_first, gain_second, bias_second, weight_second):
    channels = gain_first.shape[0]
    clips, frames, rows, flat_width = latents.shape
    shaped = latents.reshape(clips, frames, rows, flat_width // channels, channels)
    frame_index = jnp.arange(frames, dtype=jnp.int32)
    valid = frame_index[None, :] < frame_counts[:, None]
    frame_mask = valid[:, :, None, None, None]
    masked_input = jnp.where(frame_mask, shaped, jnp.zeros_like(shaped))
    normed_first = norm_silu(masked_input, gain_first)
    hidden_first = jnp.where(frame_mask, causal_conv(normed_first, weight_first) + bias_first, 0.0).astype(jnp.bfloat16)
    normed_second = norm_silu(hidden_first, gain_second)
    summed = masked_input.astype(jnp.float32) + causal_conv(normed_second, weight_second) + bias_second
    encoded = jnp.where(frame_mask, summed, 0.0).astype(jnp.bfloat16)
    return encoded.reshape(clips, frames, rows, flat_width)
```

```python
import functools

import jax
import jax.numpy as jnp
from jax import lax
from jax.experimental import pallas as pl
from jax.experimental.pallas import tpu as pltpu
from jax.sharding import PartitionSpec as P

MESH = pl.DeviceIdType.MESH
LANES = 128
BF16 = jnp.bfloat16
F32 = jnp.float32


def kernel(
    bands,
    blocks,
    counts_ref,
    x_hbm,
    gain1_hbm,
    bias1_hbm,
    gain2_hbm,
    bias2_hbm,
    w1_hbm,
    w2_hbm,
    out_ref,
    vectors,
    w1,
    w2,
    x_ref,
    p1,
    p2,
    own,
    halo,
    tail,
    corner,
    early,
    from_time,
    from_space,
    from_corner,
    hidden_out,
    hidden_in,
    l_sems,
    send_sems,
    recv_sems,
):
    frames, rows, width = x_ref.shape
    channels = vectors.shape[-1]
    flat = 2 * channels
    pairs = width // flat
    half = flat // 2 - LANES
    sides = 1 if bands == 2 else 2
    first_hidden = 0 if sides == 1 else -1
    hrows = rows + sides
    base1 = 1 if sides == 1 else 2
    tm = lax.axis_index("tm")
    band = lax.axis_index("space")
    has_prev = tm > 0
    has_next = tm < blocks - 1
    count = counts_ref[0]

    def both(a, b):
        return b if a is None else (a if b is None else jnp.logical_and(a, b))

    def when(cond, fn):
        if cond is None:
            fn()
        else:
            pl.when(cond)(fn)

    if sides == 1:
        flip = band
        links = [(1 - band, None, (1 - band) * (rows - 2), 0)]
        slot_cond = [None]
    else:
        flip = 0
        links = [
            (band - 1, band > 0, 0, 1),
            (band + 1, band < bands - 1, rows - 2, 0),
        ]
        slot_cond = [band > 0, band < bands - 1]

    peers = [({"space": p}, c) for p, c, _, _ in links]
    for step, has in ((1, has_next), (-1, has_prev)):
        peers.append(({"tm": tm + step}, has))
        peers += [({"tm": tm + step, "space": p}, both(c, has)) for p, c, _, _ in links]

    barrier = pltpu.get_barrier_semaphore()
    total = 0
    for device, cond in peers:
        when(
            cond,
            lambda device=device: pl.semaphore_signal(
                barrier, inc=1, device_id=device, device_id_type=MESH
            ),
        )
        total = total + (1 if cond is None else cond.astype(jnp.int32))

    load_x = pltpu.make_async_copy(x_hbm, x_ref, l_sems.at[0])
    loads = []
    for n, (source, target) in enumerate(((w1_hbm, w1), (w2_hbm, w2))):
        loads.append(
            [
                pltpu.make_async_copy(
                    source.at[:, b + flip * (2 - 2 * b)], target.at[:, b], l_sems.at[1 + 3 * n + b]
                )
                for b in range(3)
            ]
        )
    small = [
        pltpu.make_async_copy(source, vectors.at[i], l_sems.at[7 + i])
        for i, source in enumerate((gain1_hbm, bias1_hbm, gain2_hbm, bias2_hbm))
    ]
    load_x.start()
    for copy in small:
        copy.start()
    for copy in loads[0] + loads[1]:
        copy.start()

    def fill(ref):
        ref[...] = jnp.zeros(ref.shape, ref.dtype)

    pad = jnp.zeros((frames + 2, 1) + p1.shape[2:], BF16)
    if sides == 1:
        p1[:, 0:1] = pad
        p2[:, 0:1] = pad

    def no_prev():
        fill(from_time)
        fill(from_corner)
        for ref in hidden_in:
            fill(ref)

    pl.when(jnp.logical_not(has_prev))(no_prev)
    if sides == 2:
        for slot in range(2):

            def outside(slot=slot):
                from_space[slot] = jnp.zeros(from_space.shape[1:], BF16)

            def outside_corner(slot=slot):
                from_corner[slot] = jnp.zeros(from_corner.shape[1:], BF16)

            pl.when(jnp.logical_not(slot_cond[slot]))(outside)
            pl.when(jnp.logical_and(jnp.logical_not(slot_cond[slot]), has_prev))(outside_corner)

    load_x.wait()
    pl.semaphore_wait(barrier, total)

    def remote(src, dst, at, device):
        return pltpu.make_async_remote_copy(
            src_ref=src,
            dst_ref=dst,
            send_sem=send_sems.at[at],
            recv_sem=recv_sems.at[at],
            device_id=device,
            device_id_type=MESH,
        )

    last = pl.ds(frames - 2, 2)
    sends = []
    for peer, cond, edge, slot in links:
        copy = remote(x_ref.at[:, pl.ds(edge, 2)], from_space.at[slot], slot, {"space": peer})
        sends.append((copy, cond))
    time_copy = remote(x_ref.at[last], from_time, 4, {"tm": tm + 1})
    sends.append((time_copy, has_next))
    for peer, cond, edge, slot in links:
        copy = remote(
            x_ref.at[last, pl.ds(edge, 2)],
            from_corner.at[slot],
            2 + slot,
            {"tm": tm + 1, "space": peer},
        )
        sends.append((copy, both(cond, has_next)))
    for copy, cond in sends:
        when(cond, copy.start)

    first = tm * frames
    lane = lax.broadcasted_iota(jnp.int32, (pairs, LANES), 1)
    pair = lax.broadcasted_iota(jnp.int32, (pairs, LANES), 0)
    low = lane < half

    def wide(i):
        value = vectors[i]
        return jnp.concatenate([value, value], axis=-1)

    def scale_of(gain, frame_at):
        return gain * jnp.where(first - 2 + frame_at < count, 1.0, 0.0)

    def natural(row, size):
        if sides == 2:
            return row
        return row + flip * (size - 1 - 2 * row)

    def spread(source, rows_in, target):
        for p in range(pairs):
            for i in range(3):
                at = p * flat + i * LANES
                part = source[:, at : at + LANES].astype(F32)
                target.at[i][pl.ds(p, rows_in, stride=pairs), :] = part

    def row_at(ref, row, size):
        start = natural(row, size) * pairs
        if not isinstance(start, int):
            start = pl.multiple_of(start, pairs)
        return jnp.concatenate([ref[i, pl.ds(start, pairs), :] for i in range(3)], axis=-1)

    def before(v):
        return jnp.where(pair > 0, pltpu.roll(v, 1, 0), 0.0)

    def after(v):
        return jnp.where(pair < pairs - 1, pltpu.roll(v, pairs - 1, 0), 0.0)

    def put(plane, tiles, frame_at, row_index, with_tiles=True):
        v0, v1, v2 = tiles
        mixed = jnp.where(low, after(v1), before(v1))
        for i, v in enumerate((v0, v1, v2, after(v0), before(v2), mixed)):
            plane[frame_at, row_index, :, i * LANES : (i + 1) * LANES] = v.astype(BF16)

    def tiles_of(value):
        return [value[:, i * LANES : (i + 1) * LANES] for i in range(3)]

    def norm(value, scale):
        v0, v1, v2 = tiles_of(value)
        s1 = v1 * v1
        even = jnp.sum(v0 * v0 + jnp.where(low, s1, 0.0), axis=-1, keepdims=True)
        odd = jnp.sum(v2 * v2 + jnp.where(low, 0.0, s1), axis=-1, keepdims=True)
        even = lax.rsqrt(even * (1.0 / channels) + 1e-06)
        odd = lax.rsqrt(odd * (1.0 / channels) + 1e-06)
        out = []
        for i, (v, inverse) in enumerate(((v0, even), (v1, jnp.where(low, even, odd)), (v2, odd))):
            scaled = v * inverse * scale[:, i * LANES : (i + 1) * LANES]
            out.append(scaled * jax.nn.sigmoid(scaled))
        return out

    def conv(plane, w, frame_at, nf, row_index, nr, taps):
        even, odd = None, None

        def add(acc, lhs, rhs):
            term = jnp.dot(lhs, rhs, preferred_element_type=F32)
            return term if acc is None else acc + term

        rest = LANES - half
        zero = jnp.zeros((half, channels), BF16)
        held = []
        for a in taps:
            for b in range(3):

                def tile(i, n=1, a=a, b=b):
                    value = plane[
                        frame_at + a : frame_at + a + nf,
                        row_index + b : row_index + b + nr,
                        :,
                        i * LANES : (i + n) * LANES,
                    ]
                    return value.reshape(nf * nr * pairs, n * LANES)

                k0, k1, k2 = [w.at[a, b, e] for e in range(3)]
                main = tile(0, 2)
                third = tile(2)
                even = add(even, main, jnp.concatenate([k1[...], k2[:half]], axis=0))
                odd = add(odd, main, jnp.concatenate([k0[...], k1[:half]], axis=0))
                even = add(
                    even,
                    jnp.concatenate([third, tile(4)], axis=-1),
                    jnp.concatenate([k2[half:], k0[half:]], axis=0),
                )
                odd = add(
                    odd,
                    jnp.concatenate([third, tile(3)], axis=-1),
                    jnp.concatenate([k1[half:], k2[:LANES]], axis=0),
                )
                held.append((tile(5), [zero, k0[:half]], [k2[LANES:], zero]))
                if len(held) == 2 or (a == taps[-1] and b == 2):
                    lhs = jnp.concatenate([h[0] for h in held], axis=-1)
                    even = add(even, lhs, jnp.concatenate(sum([h[1] for h in held], []), axis=0))
                    odd = add(odd, lhs, jnp.concatenate(sum([h[2] for h in held], []), axis=0))
                    held = []
        return jnp.concatenate([even, odd], axis=-1)

    def piece(value, n):
        return value[n * pairs : (n + 1) * pairs]

    def put_rows(source, rows_in, target, frame_at, row_list):
        spread(source, rows_in, target)
        scale = scale_of(gain1, frame_at)
        for row, row_index in row_list:
            put(p1, norm(row_at(target, row, rows_in), scale), frame_at, row_index)

    def hidden(frame_at, nf, row, nr, saved=None):
        summed = conv(p1, w1, frame_at, nf, row - 1 + base1, nr, (0, 1, 2)) + bias1
        rounded = summed.astype(BF16).astype(F32)
        for f in range(nf):
            scale = scale_of(gain2, frame_at + f + 2)
            for r in range(nr):
                at = row + r
                inside = scale
                if sides == 2 and (at < 0 or at >= rows):
                    inside = scale * jnp.where(slot_cond[0 if at < 0 else 1], 1.0, 0.0)
                tiles = norm(piece(rounded, f * nr + r), inside)
                put(p2, tiles, frame_at + f + 2, at + 1)
                if saved is not None:
                    for i, v in enumerate(tiles):
                        saved[f, r, :, i * LANES : (i + 1) * LANES] = v.astype(BF16)

    def settle(f, values):
        valid = jnp.where(first + f < count, 1.0, 0.0)
        for r in range(rows):
            start = natural(r, rows) * pairs
            if not isinstance(start, int):
                start = pl.multiple_of(start, pairs)
            for i, v in enumerate(tiles_of(values[r] * valid)):
                own[f, i, pl.ds(start, pairs), :] = v
        for p in range(pairs):
            for i in range(3):
                value = own.at[f, i][pl.ds(p, rows, stride=pairs), :]
                at = p * flat + i * LANES
                out_ref[f, :, at : at + LANES] = value.astype(BF16)

    def with_input(f, summed):
        return [piece(summed, r) + row_at(own.at[f], r, rows) for r in range(rows)]

    for copy in small:
        copy.wait()
    gain1, bias1, gain2, bias2 = [wide(i) for i in range(4)]
    for f in range(frames):
        put_rows(x_ref.at[f], rows, own.at[f], f + 2, [(r, r + base1) for r in range(rows)])
    for copy in loads[0]:
        copy.wait()
    hidden_copies = []
    if sides == 1:
        parts = [(0, rows - 1), (rows - 1, 2)]
    else:
        parts = [(first_hidden, hrows)]
    for n in range(len(parts)):
        hidden_copies.append(remote(hidden_out[n], hidden_in[n], 5 + n, {"tm": tm + 1}))
    if sides == 1:
        hidden(frames - 2, 2, *parts[0], hidden_out[0])
        when(has_next, hidden_copies[0].start)

    def halo_rows(slot):
        if sides == 1:
            return [(0, rows + base1), (1, rows + 1 + base1)]
        at = 0 if slot == 0 else rows + 2
        return [(0, at), (1, at + 1)]

    for slot in range(sides):
        landed = remote(
            x_ref.at[:, pl.ds(0, 2)], from_space.at[slot], slot, {"space": band}
        )
        when(slot_cond[slot], landed.wait_recv)
        for f in range(frames):
            put_rows(from_space.at[slot, f], 2, halo.at[slot, f], f + 2, halo_rows(slot))
    hidden(frames - 2, 2, *parts[-1], hidden_out[-1])
    when(has_next, hidden_copies[-1].start)

    pl.when(has_prev)(time_copy.wait_recv)
    for slot in range(sides):
        landed = remote(
            x_ref.at[last, pl.ds(0, 2)], from_corner.at[slot], 2 + slot, {"space": band}
        )
        when(both(slot_cond[slot], has_prev), landed.wait_recv)
    for f in range(2):
        put_rows(from_time.at[f], rows, tail.at[f], f, [(r, r + base1) for r in range(rows)])
        for slot in range(sides):
            put_rows(from_corner.at[slot, f], 2, corner.at[slot, f], f, halo_rows(slot))

    hidden(0, frames - 2, first_hidden, hrows)
    for copy in loads[1]:
        copy.wait()
    summed = conv(p2, w2, frames - 2, 2, 0, rows, (0, 1, 2)) + bias2
    for f in range(2):
        settle(
            frames - 2 + f,
            with_input(frames - 2 + f, summed[f * rows * pairs : (f + 1) * rows * pairs]),
        )
    for f, taps in ((0, (2,)), (1, (1, 2))):
        values = with_input(f, conv(p2, w2, f, 1, 0, rows, taps) + bias2)
        for r in range(rows):
            early[f, r] = values[r]

    for copy in hidden_copies:
        pl.when(has_prev)(copy.wait_recv)
    for (row, nr), ref in zip(parts, hidden_in):
        for f in range(2):
            for r in range(nr):
                put(p2, tiles_of(ref[f, r].astype(F32)), f, row + r + 1)
    for f, taps in ((0, (0, 1)), (1, (0,))):
        summed = conv(p2, w2, f, 1, 0, rows, taps)
        settle(f, [piece(summed, r) + early[f, r] for r in range(rows)])
    for copy, cond in sends + [(c, has_next) for c in hidden_copies]:
        when(cond, copy.wait_send)


def shards(
    bands,
    blocks,
    latents,
    frame_counts,
    gain_first,
    bias_first,
    weight_first,
    gain_second,
    bias_second,
    weight_second,
):
    channels = gain_first.shape[0]
    frames, rows, width = latents.shape[1:]
    flat = 2 * channels
    pairs = width // flat
    x = latents.reshape(frames, rows, width)
    sides = 1 if bands == 2 else 2
    vmem = pl.BlockSpec(memory_space=pltpu.VMEM)
    hbm = pl.BlockSpec(memory_space=pltpu.HBM)
    parts = [rows - 1, 2] if sides == 1 else [rows + 2]
    scratch = pltpu.VMEM
    rows1 = rows + (3 if sides == 1 else 4)
    out = pl.pallas_call(
        functools.partial(kernel, bands, blocks),
        out_shape=pltpu.VMEM(x.shape, BF16),
        in_specs=[pl.BlockSpec(memory_space=pltpu.SMEM)] + [hbm] * 7,
        out_specs=vmem,
        scratch_shapes=[
            scratch((4, 1, channels), F32),
            scratch((3, 3, 3, channels, channels), BF16),
            scratch((3, 3, 3, channels, channels), BF16),
            scratch(x.shape, BF16),
            scratch((frames + 2, rows1, pairs, 6 * LANES), BF16),
            scratch((frames + 2, rows + 2, pairs, 6 * LANES), BF16),
            scratch((frames, 3, rows * pairs, LANES), F32),
            scratch((sides, frames, 3, 2 * pairs, LANES), F32),
            scratch((2, 3, rows * pairs, LANES), F32),
            scratch((sides, 2, 3, 2 * pairs, LANES), F32),
            scratch((2, rows, pairs, flat), F32),
            scratch((2, rows, width), BF16),
            scratch((sides, frames, 2, width), BF16),
            scratch((sides, 2, 2, width), BF16),
            [scratch((2, n, pairs, flat), BF16) for n in parts],
            [scratch((2, n, pairs, flat), BF16) for n in parts],
            pltpu.SemaphoreType.DMA((11,)),
            pltpu.SemaphoreType.DMA((7,)),
            pltpu.SemaphoreType.DMA((7,)),
        ],
        compiler_params=pltpu.CompilerParams(
            collective_id=0, has_side_effects=True, vmem_limit_bytes=40 * 1024 * 1024
        ),
    )(
        frame_counts,
        pltpu.with_memory_space_constraint(x, pltpu.HBM),
        pltpu.with_memory_space_constraint(gain_first.reshape(1, channels), pltpu.HBM),
        pltpu.with_memory_space_constraint(bias_first.reshape(1, channels), pltpu.HBM),
        pltpu.with_memory_space_constraint(gain_second.reshape(1, channels), pltpu.HBM),
        pltpu.with_memory_space_constraint(bias_second.reshape(1, channels), pltpu.HBM),
        pltpu.with_memory_space_constraint(weight_first, pltpu.HBM),
        pltpu.with_memory_space_constraint(weight_second, pltpu.HBM),
    )
    return out.reshape(latents.shape)


def solution(mesh):
    return jax.shard_map(
        functools.partial(shards, mesh.shape["space"], mesh.shape["tm"]),
        mesh=mesh,
        in_specs=(P(("groups", "clip"), "tm", "space", None), P(("groups", "clip"))) + (P(),) * 6,
        out_specs=P(("groups", "clip"), "tm", "space", None),
        check_vma=False,
    )
```

```python
import functools

import jax
import jax.numpy as jnp
from jax import lax
from jax.experimental import pallas as pl
from jax.experimental.pallas import tpu as pltpu
from jax.sharding import PartitionSpec as P

MESH = pl.DeviceIdType.MESH
LANES = 128
BF16 = jnp.bfloat16
F32 = jnp.float32


def kernel(
    bands,
    blocks,
    counts_ref,
    x_hbm,
    gain1_hbm,
    bias1_hbm,
    gain2_hbm,
    bias2_hbm,
    w1_hbm,
    w2_hbm,
    out_ref,
    vectors,
    w1,
    w2,
    x_ref,
    p1,
    p2,
    own,
    halo,
    tail,
    corner,
    early,
    from_time,
    from_space,
    from_corner,
    hidden_out,
    hidden_in,
    l_sems,
    send_sems,
    recv_sems,
):
    frames, rows, width = x_ref.shape
    channels = vectors.shape[-1]
    flat = 2 * channels
    pairs = width // flat
    half = flat // 2 - LANES
    sides = 1 if bands == 2 else 2
    first_hidden = 0 if sides == 1 else -1
    hrows = rows + sides
    base1 = 1 if sides == 1 else 2
    tm = lax.axis_index("tm")
    band = lax.axis_index("space")
    has_prev = tm > 0
    has_next = tm < blocks - 1

    def both(a, b):
        return b if a is None else (a if b is None else jnp.logical_and(a, b))

    def when(cond, fn):
        if cond is None:
            fn()
        else:
            pl.when(cond)(fn)

    if sides == 1:
        flip = band
        links = [(1 - band, None, (1 - band) * (rows - 2), 0)]
        slot_cond = [None]
    else:
        flip = 0
        links = [
            (band - 1, band > 0, 0, 1),
            (band + 1, band < bands - 1, rows - 2, 0),
        ]
        slot_cond = [band > 0, band < bands - 1]

    peers = [({"space": p}, c) for p, c, _, _ in links]
    for step, has in ((1, has_next), (-1, has_prev)):
        peers.append(({"tm": tm + step}, has))
        peers += [({"tm": tm + step, "space": p}, both(c, has)) for p, c, _, _ in links]

    barrier = pltpu.get_barrier_semaphore()
    total = 0
    for device, cond in peers:
        when(
            cond,
            lambda device=device: pl.semaphore_signal(
                barrier, inc=1, device_id=device, device_id_type=MESH
            ),
        )
        total = total + (1 if cond is None else cond.astype(jnp.int32))

    load_x = pltpu.make_async_copy(x_hbm, x_ref, l_sems.at[0])
    loads = []
    for n, (source, target) in enumerate(((w1_hbm, w1), (w2_hbm, w2))):
        loads.append(
            [
                pltpu.make_async_copy(
                    source.at[:, b + flip * (2 - 2 * b)], target.at[:, b], l_sems.at[1 + 3 * n + b]
                )
                for b in range(3)
            ]
        )
    small = [
        pltpu.make_async_copy(source, vectors.at[i], l_sems.at[7 + i])
        for i, source in enumerate((gain1_hbm, bias1_hbm, gain2_hbm, bias2_hbm))
    ]
    load_x.start()
    for copy in small:
        copy.start()
    for copy in loads[0] + loads[1]:
        copy.start()

    def fill(ref):
        ref[...] = jnp.zeros(ref.shape, ref.dtype)

    if sides == 1:
        pad = jnp.zeros((frames + 2, 1) + p1.shape[2:], BF16)
        p1[:, 0:1] = pad
        p2[:, 0:1] = pad
    for plane in (p1, p2):
        for i in (4, 9):
            top = plane.shape[1] - 1
            plane[:, top : top + 1, :, i * LANES : (i + 1) * LANES] = jnp.zeros(
                (frames + 2, 1, pairs, LANES), BF16
            )

    def no_prev():
        fill(from_time)
        fill(from_corner)
        for ref in hidden_in:
            fill(ref)

    pl.when(jnp.logical_not(has_prev))(no_prev)
    if sides == 2:
        for slot in range(2):

            def outside(slot=slot):
                from_space[slot] = jnp.zeros(from_space.shape[1:], BF16)

            def outside_corner(slot=slot):
                from_corner[slot] = jnp.zeros(from_corner.shape[1:], BF16)

            pl.when(jnp.logical_not(slot_cond[slot]))(outside)
            pl.when(jnp.logical_and(jnp.logical_not(slot_cond[slot]), has_prev))(outside_corner)

    load_x.wait()
    pl.semaphore_wait(barrier, total)

    def remote(src, dst, at, device):
        return pltpu.make_async_remote_copy(
            src_ref=src,
            dst_ref=dst,
            send_sem=send_sems.at[at],
            recv_sem=recv_sems.at[at],
            device_id=device,
            device_id_type=MESH,
        )

    last = pl.ds(frames - 2, 2)
    sends = []
    for peer, cond, edge, slot in links:
        copy = remote(x_ref.at[:, pl.ds(edge, 2)], from_space.at[slot], slot, {"space": peer})
        sends.append((copy, cond))
    time_copy = remote(x_ref.at[last], from_time, 4, {"tm": tm + 1})
    sends.append((time_copy, has_next))
    for peer, cond, edge, slot in links:
        copy = remote(
            x_ref.at[last, pl.ds(edge, 2)],
            from_corner.at[slot],
            2 + slot,
            {"tm": tm + 1, "space": peer},
        )
        sends.append((copy, both(cond, has_next)))
    for copy, cond in sends:
        when(cond, copy.start)

    first = tm * frames
    lane = lax.broadcasted_iota(jnp.int32, (pairs, LANES), 1)
    pair = lax.broadcasted_iota(jnp.int32, (pairs, LANES), 0)
    low = lane < half

    def wide(i):
        value = vectors[i]
        return jnp.concatenate([value, value], axis=-1)

    def scale_of(gain, frame_at):
        return gain * jnp.where(first - 2 + frame_at < count, 1.0, 0.0)

    def natural(row, size):
        if sides == 2:
            return row
        return row + flip * (size - 1 - 2 * row)

    def spread(source, rows_in, target):
        for p in range(pairs):
            for i in range(3):
                at = p * flat + i * LANES
                part = source[:, at : at + LANES].astype(F32)
                target.at[i][pl.ds(p, rows_in, stride=pairs), :] = part

    def row_at(ref, row, size):
        start = natural(row, size) * pairs
        if not isinstance(start, int):
            start = pl.multiple_of(start, pairs)
        return jnp.concatenate([ref[i, pl.ds(start, pairs), :] for i in range(3)], axis=-1)

    def before(v):
        return jnp.where(pair > 0, pltpu.roll(v, 1, 0), 0.0)

    def after(v):
        return jnp.where(pair < pairs - 1, pltpu.roll(v, pairs - 1, 0), 0.0)

    def put(plane, tiles, frame_at, row_index):
        v0, v1, v2 = tiles
        r0, r1, r2 = [pltpu.roll(v, half, 1) for v in tiles]
        joint = jnp.where(low, r1, r2)
        nearby = after(v1)
        even = (before(joint), jnp.where(low, before(r2), r0), jnp.where(low, r0, r1), joint)
        odd = (v0, v1, v2, after(v0))
        for n, (values, end, raised) in enumerate(
            ((even, r2, v2), (odd, nearby, pltpu.roll(nearby, half, 1)))
        ):
            at = 5 * n * LANES
            for i, v in enumerate(values):
                plane[frame_at, row_index, :, at + i * LANES : at + (i + 1) * LANES] = v.astype(BF16)
            at += 4 * LANES
            plane[frame_at, row_index, :, at : at + half] = end[:, :half].astype(BF16)
            if row_index > 0:
                plane[frame_at, row_index - 1, :, at + half : at + LANES] = raised[:, half:].astype(
                    BF16
                )

    def tiles_of(value):
        return [value[:, i * LANES : (i + 1) * LANES] for i in range(3)]

    def norm(value, scale):
        v0, v1, v2 = tiles_of(value)
        s1 = v1 * v1
        even = jnp.sum(v0 * v0 + jnp.where(low, s1, 0.0), axis=-1, keepdims=True)
        odd = jnp.sum(v2 * v2 + jnp.where(low, 0.0, s1), axis=-1, keepdims=True)
        even = lax.rsqrt(even * (1.0 / channels) + 1e-06)
        odd = lax.rsqrt(odd * (1.0 / channels) + 1e-06)
        out = []
        for i, (v, inverse) in enumerate(((v0, even), (v1, jnp.where(low, even, odd)), (v2, odd))):
            scaled = v * inverse * scale[:, i * LANES : (i + 1) * LANES]
            out.append(scaled * jax.nn.sigmoid(scaled))
        return out

    def conv(plane, w, frame_at, nf, row_index, nr, taps):
        chains = [None, None]
        size = nf * nr * pairs
        done = 0
        zero = jnp.zeros((half, channels), BF16)

        def tile(a, b, i, n):
            both_columns = []
            for c in range(2):
                at = (5 * c + i) * LANES
                value = plane[
                    frame_at + a : frame_at + a + nf,
                    row_index + b : row_index + b + nr,
                    :,
                    at : at + n * LANES,
                ]
                both_columns.append(value.reshape(size, n * LANES))
            return jnp.concatenate(both_columns, axis=0)

        for a in taps:
            terms = []
            for b in range(3):
                for n in range(2):
                    terms.append(
                        (tile(a, b, 2 * n, 2), w[a, b, 2 * n * LANES : 2 * (n + 1) * LANES])
                    )
            ends = [w[a, b, 4 * LANES :] for b in range(3)] + [zero]
            terms.append(
                (
                    jnp.concatenate([tile(a, 0, 4, 1), tile(a, 2, 4, 1)], axis=-1),
                    jnp.concatenate(ends, axis=0),
                )
            )
            for lhs, rhs in terms:
                term = jnp.dot(lhs, rhs, preferred_element_type=F32)
                n = done % 2
                chains[n] = term if chains[n] is None else chains[n] + term
                done += 1
        a, b = [jnp.concatenate([c[:size], c[size:]], axis=-1) for c in chains]
        return a + b

    def piece(value, n):
        return value[n * pairs : (n + 1) * pairs]

    def put_rows(source, rows_in, target, frame_at, row_list):
        spread(source, rows_in, target)
        scale = scale_of(gain1, frame_at)
        for row, row_index in row_list:
            put(p1, norm(row_at(target, row, rows_in), scale), frame_at, row_index)

    def hidden(frame_at, nf, row, nr, saved=None):
        summed = conv(p1, w1, frame_at, nf, row - 1 + base1, nr, (0, 1, 2)) + bias1
        rounded = summed.astype(BF16).astype(F32)
        for f in range(nf):
            scale = scale_of(gain2, frame_at + f + 2)
            for r in range(nr):
                at = row + r
                inside = scale
                if sides == 2 and (at < 0 or at >= rows):
                    inside = scale * jnp.where(slot_cond[0 if at < 0 else 1], 1.0, 0.0)
                tiles = norm(piece(rounded, f * nr + r), inside)
                put(p2, tiles, frame_at + f + 2, at + 1)
                if saved is not None:
                    for i, v in enumerate(tiles):
                        saved[f, r, :, i * LANES : (i + 1) * LANES] = v.astype(BF16)

    def settle(f, values):
        valid = jnp.where(first + f < count, 1.0, 0.0)
        for r in range(rows):
            start = natural(r, rows) * pairs
            if not isinstance(start, int):
                start = pl.multiple_of(start, pairs)
            for i, v in enumerate(tiles_of(values[r] * valid)):
                own[f, i, pl.ds(start, pairs), :] = v
        for p in range(pairs):
            for i in range(3):
                value = own.at[f, i][pl.ds(p, rows, stride=pairs), :]
                at = p * flat + i * LANES
                out_ref[f, :, at : at + LANES] = value.astype(BF16)

    def with_input(f, summed):
        return [piece(summed, r) + row_at(own.at[f], r, rows) for r in range(rows)]

    count = counts_ref[0]
    for copy in small:
        copy.wait()
    gain1, bias1, gain2, bias2 = [wide(i) for i in range(4)]
    for f in range(frames):
        put_rows(x_ref.at[f], rows, own.at[f], f + 2, [(r, r + base1) for r in range(rows)])
    for copy in loads[0]:
        copy.wait()
    hidden_copies = []
    if sides == 1:
        parts = [(0, rows - 1), (rows - 1, 2)]
    else:
        parts = [(first_hidden, hrows)]
    for n in range(len(parts)):
        hidden_copies.append(remote(hidden_out[n], hidden_in[n], 5 + n, {"tm": tm + 1}))
    if sides == 1:
        hidden(frames - 2, 2, *parts[0], hidden_out[0])
        when(has_next, hidden_copies[0].start)

    def halo_rows(slot):
        if sides == 1:
            return [(0, rows + base1), (1, rows + 1 + base1)]
        at = 0 if slot == 0 else rows + 2
        return [(0, at), (1, at + 1)]

    for slot in range(sides):
        landed = remote(
            x_ref.at[:, pl.ds(0, 2)], from_space.at[slot], slot, {"space": band}
        )
        when(slot_cond[slot], landed.wait_recv)
        for f in range(frames):
            put_rows(from_space.at[slot, f], 2, halo.at[slot, f], f + 2, halo_rows(slot))
    hidden(frames - 2, 2, *parts[-1], hidden_out[-1])
    when(has_next, hidden_copies[-1].start)

    pl.when(has_prev)(time_copy.wait_recv)
    for slot in range(sides):
        landed = remote(
            x_ref.at[last, pl.ds(0, 2)], from_corner.at[slot], 2 + slot, {"space": band}
        )
        when(both(slot_cond[slot], has_prev), landed.wait_recv)
    for f in range(2):
        put_rows(from_time.at[f], rows, tail.at[f], f, [(r, r + base1) for r in range(rows)])
        for slot in range(sides):
            put_rows(from_corner.at[slot, f], 2, corner.at[slot, f], f, halo_rows(slot))

    hidden(0, frames - 2, first_hidden, hrows)
    for copy in loads[1]:
        copy.wait()
    summed = conv(p2, w2, frames - 2, 2, 0, rows, (0, 1, 2)) + bias2
    for f in range(2):
        settle(
            frames - 2 + f,
            with_input(frames - 2 + f, summed[f * rows * pairs : (f + 1) * rows * pairs]),
        )
    shared = conv(p2, w2, 0, 2, 0, rows, (2,)) + bias2
    single = conv(p2, w2, 1, 1, 0, rows, (1,))
    for f in range(2):
        value = shared[f * rows * pairs : (f + 1) * rows * pairs]
        values = with_input(f, value + single if f == 1 else value)
        for r in range(rows):
            early[f, r] = values[r]

    for copy in hidden_copies:
        pl.when(has_prev)(copy.wait_recv)
    for (row, nr), ref in zip(parts, hidden_in):
        for f in range(2):
            for r in range(nr):
                put(p2, tiles_of(ref[f, r].astype(F32)), f, row + r + 1)
    shared = conv(p2, w2, 0, 2, 0, rows, (0,))
    single = conv(p2, w2, 0, 1, 0, rows, (1,))
    for f in range(2):
        value = shared[f * rows * pairs : (f + 1) * rows * pairs]
        summed = value + single if f == 0 else value
        settle(f, [piece(summed, r) + early[f, r] for r in range(rows)])
    for copy, cond in sends + [(c, has_next) for c in hidden_copies]:
        when(cond, copy.wait_send)


def shards(
    bands,
    blocks,
    latents,
    frame_counts,
    gain_first,
    bias_first,
    weight_first,
    gain_second,
    bias_second,
    weight_second,
):
    channels = gain_first.shape[0]
    frames, rows, width = latents.shape[1:]
    flat = 2 * channels
    pairs = width // flat
    x = latents.reshape(frames, rows, width)
    sides = 1 if bands == 2 else 2
    vmem = pl.BlockSpec(memory_space=pltpu.VMEM)
    hbm = pl.BlockSpec(memory_space=pltpu.HBM)
    parts = [rows - 1, 2] if sides == 1 else [rows + 2]
    scratch = pltpu.VMEM
    taps = (3, 3, 3 * channels, channels)
    rows1 = rows + (3 if sides == 1 else 4)
    out = pl.pallas_call(
        functools.partial(kernel, bands, blocks),
        out_shape=pltpu.VMEM(x.shape, BF16),
        in_specs=[pl.BlockSpec(memory_space=pltpu.SMEM)] + [hbm] * 7,
        out_specs=vmem,
        scratch_shapes=[
            scratch((4, 1, channels), F32),
            scratch((3, 3, 3 * channels, channels), BF16),
            scratch((3, 3, 3 * channels, channels), BF16),
            scratch(x.shape, BF16),
            scratch((frames + 2, rows1, pairs, 10 * LANES), BF16),
            scratch((frames + 2, rows + 2, pairs, 10 * LANES), BF16),
            scratch((frames, 3, rows * pairs, LANES), F32),
            scratch((sides, frames, 3, 2 * pairs, LANES), F32),
            scratch((2, 3, rows * pairs, LANES), F32),
            scratch((sides, 2, 3, 2 * pairs, LANES), F32),
            scratch((2, rows, pairs, flat), F32),
            scratch((2, rows, width), BF16),
            scratch((sides, frames, 2, width), BF16),
            scratch((sides, 2, 2, width), BF16),
            [scratch((2, n, pairs, flat), BF16) for n in parts],
            [scratch((2, n, pairs, flat), BF16) for n in parts],
            pltpu.SemaphoreType.DMA((11,)),
            pltpu.SemaphoreType.DMA((7,)),
            pltpu.SemaphoreType.DMA((7,)),
        ],
        compiler_params=pltpu.CompilerParams(
            collective_id=0, has_side_effects=True, vmem_limit_bytes=40 * 1024 * 1024
        ),
    )(
        frame_counts,
        pltpu.with_memory_space_constraint(x, pltpu.HBM),
        pltpu.with_memory_space_constraint(gain_first.reshape(1, channels), pltpu.HBM),
        pltpu.with_memory_space_constraint(bias_first.reshape(1, channels), pltpu.HBM),
        pltpu.with_memory_space_constraint(gain_second.reshape(1, channels), pltpu.HBM),
        pltpu.with_memory_space_constraint(bias_second.reshape(1, channels), pltpu.HBM),
        pltpu.with_memory_space_constraint(weight_first.reshape(taps), pltpu.HBM),
        pltpu.with_memory_space_constraint(weight_second.reshape(taps), pltpu.HBM),
    )
    return out.reshape(latents.shape)


def solution(mesh):
    return jax.shard_map(
        functools.partial(shards, mesh.shape["space"], mesh.shape["tm"]),
        mesh=mesh,
        in_specs=(P(("groups", "clip"), "tm", "space", None), P(("groups", "clip"))) + (P(),) * 6,
        out_specs=P(("groups", "clip"), "tm", "space", None),
        check_vma=False,
    )
```

```python
import functools

import jax
import jax.numpy as jnp
from jax import lax
from jax.experimental import pallas as pl
from jax.experimental.pallas import tpu as pltpu
from jax.sharding import PartitionSpec as P

MESH = pl.DeviceIdType.MESH
LANES = 128
BF16 = jnp.bfloat16
F32 = jnp.float32


def kernel(
    bands,
    blocks,
    counts_ref,
    x_hbm,
    gain1_hbm,
    bias1_hbm,
    gain2_hbm,
    bias2_hbm,
    w1_hbm,
    w2_hbm,
    out_ref,
    vectors,
    w1,
    w2,
    x_ref,
    p1,
    p2,
    own,
    halo,
    tail,
    corner,
    early,
    from_time,
    from_space,
    from_corner,
    hidden_out,
    hidden_in,
    l_sems,
    send_sems,
    recv_sems,
):
    frames, rows, width = x_ref.shape
    channels = vectors.shape[-1]
    flat = 2 * channels
    pairs = width // flat
    half = flat // 2 - LANES
    sides = 1 if bands == 2 else 2
    first_hidden = 0 if sides == 1 else -1
    hrows = rows + sides
    base1 = 1 if sides == 1 else 2
    tm = lax.axis_index("tm")
    band = lax.axis_index("space")
    has_prev = tm > 0
    has_next = tm < blocks - 1

    def both(a, b):
        return b if a is None else (a if b is None else jnp.logical_and(a, b))

    def when(cond, fn):
        if cond is None:
            fn()
        else:
            pl.when(cond)(fn)

    if sides == 1:
        flip = band
        links = [(1 - band, None, (1 - band) * (rows - 2), 0)]
        slot_cond = [None]
    else:
        flip = 0
        links = [
            (band - 1, band > 0, 0, 1),
            (band + 1, band < bands - 1, rows - 2, 0),
        ]
        slot_cond = [band > 0, band < bands - 1]

    peers = [({"space": p}, c) for p, c, _, _ in links]
    for step, has in ((1, has_next), (-1, has_prev)):
        peers.append(({"tm": tm + step}, has))
        peers += [({"tm": tm + step, "space": p}, both(c, has)) for p, c, _, _ in links]

    barrier = pltpu.get_barrier_semaphore()
    total = 0
    for device, cond in peers:
        when(
            cond,
            lambda device=device: pl.semaphore_signal(
                barrier, inc=1, device_id=device, device_id_type=MESH
            ),
        )
        total = total + (1 if cond is None else cond.astype(jnp.int32))

    load_x = pltpu.make_async_copy(x_hbm, x_ref, l_sems.at[0])
    loads = []
    for n, (source, target) in enumerate(((w1_hbm, w1), (w2_hbm, w2))):
        loads.append(
            [
                pltpu.make_async_copy(
                    source.at[:, b + flip * (2 - 2 * b)], target.at[:, b], l_sems.at[1 + 3 * n + b]
                )
                for b in range(3)
            ]
        )
    small = [
        pltpu.make_async_copy(source, vectors.at[i], l_sems.at[7 + i])
        for i, source in enumerate((gain1_hbm, bias1_hbm, gain2_hbm, bias2_hbm))
    ]
    load_x.start()
    for copy in small:
        copy.start()
    for copy in loads[0] + loads[1]:
        copy.start()

    def fill(ref):
        ref[...] = jnp.zeros(ref.shape, ref.dtype)

    if sides == 1:
        pad = jnp.zeros((frames + 2, 1) + p1.shape[2:], BF16)
        p1[:, 0:1] = pad
        p2[:, 0:1] = pad
    for plane in (p1, p2):
        for i in (4, 9):
            top = plane.shape[1] - 1
            plane[:, top : top + 1, :, i * LANES : (i + 1) * LANES] = jnp.zeros(
                (frames + 2, 1, pairs, LANES), BF16
            )

    def no_prev():
        p1[0:2] = jnp.zeros((2,) + p1.shape[1:], BF16)

    pl.when(jnp.logical_not(has_prev))(no_prev)
    if sides == 2:
        for slot in range(2):

            def outside(slot=slot):
                from_space[slot] = jnp.zeros(from_space.shape[1:], BF16)

            def outside_corner(slot=slot):
                from_corner[slot] = jnp.zeros(from_corner.shape[1:], BF16)

            pl.when(jnp.logical_not(slot_cond[slot]))(outside)
            pl.when(jnp.logical_and(jnp.logical_not(slot_cond[slot]), has_prev))(outside_corner)

    load_x.wait()

    def remote(src, dst, at, device):
        return pltpu.make_async_remote_copy(
            src_ref=src,
            dst_ref=dst,
            send_sem=send_sems.at[at],
            recv_sem=recv_sems.at[at],
            device_id=device,
            device_id_type=MESH,
        )

    last = pl.ds(frames - 2, 2)
    sends = []
    for peer, cond, edge, slot in links:
        copy = remote(x_ref.at[:, pl.ds(edge, 2)], from_space.at[slot], slot, {"space": peer})
        sends.append((copy, cond))
    time_copy = remote(x_ref.at[last], from_time, 4, {"tm": tm + 1})
    sends.append((time_copy, has_next))
    for peer, cond, edge, slot in links:
        copy = remote(
            x_ref.at[last, pl.ds(edge, 2)],
            from_corner.at[slot],
            2 + slot,
            {"tm": tm + 1, "space": peer},
        )
        sends.append((copy, both(cond, has_next)))

    first = tm * frames
    lane = lax.broadcasted_iota(jnp.int32, (pairs, LANES), 1)
    pair = lax.broadcasted_iota(jnp.int32, (pairs, LANES), 0)
    low = lane < half

    def wide(i):
        value = vectors[i]
        return jnp.concatenate([value, value], axis=-1)

    def scale_of(gain, frame_at):
        return gain * jnp.where(first - 2 + frame_at < count, 1.0, 0.0)

    def natural(row, size):
        if sides == 2:
            return row
        return row + flip * (size - 1 - 2 * row)

    def spread(source, rows_in, target):
        for p in range(pairs):
            for i in range(3):
                at = p * flat + i * LANES
                part = source[:, at : at + LANES].astype(F32)
                target.at[i][pl.ds(p, rows_in, stride=pairs), :] = part

    def row_at(ref, row, size):
        start = natural(row, size) * pairs
        if not isinstance(start, int):
            start = pl.multiple_of(start, pairs)
        return jnp.concatenate([ref[i, pl.ds(start, pairs), :] for i in range(3)], axis=-1)

    def before(v):
        return jnp.where(pair > 0, pltpu.roll(v, 1, 0), 0.0)

    def after(v):
        return jnp.where(pair < pairs - 1, pltpu.roll(v, pairs - 1, 0), 0.0)

    def put(plane, tiles, frame_at, row_index):
        v0, v1, v2 = tiles
        r0, r1, r2 = [pltpu.roll(v, half, 1) for v in tiles]
        joint = jnp.where(low, r1, r2)
        nearby = after(v1)
        even = (before(joint), jnp.where(low, before(r2), r0), jnp.where(low, r0, r1), joint)
        odd = (v0, v1, v2, after(v0))
        for n, (values, end, raised) in enumerate(
            ((even, r2, v2), (odd, nearby, pltpu.roll(nearby, half, 1)))
        ):
            at = 5 * n * LANES
            for i, v in enumerate(values):
                plane[frame_at, row_index, :, at + i * LANES : at + (i + 1) * LANES] = v.astype(BF16)
            at += 4 * LANES
            plane[frame_at, row_index, :, at : at + half] = end[:, :half].astype(BF16)
            if row_index > 0:
                plane[frame_at, row_index - 1, :, at + half : at + LANES] = raised[:, half:].astype(
                    BF16
                )

    def tiles_of(value):
        return [value[:, i * LANES : (i + 1) * LANES] for i in range(3)]

    def norm(value, scale):
        v0, v1, v2 = tiles_of(value)
        s1 = v1 * v1
        even = jnp.sum(v0 * v0 + jnp.where(low, s1, 0.0), axis=-1, keepdims=True)
        odd = jnp.sum(v2 * v2 + jnp.where(low, 0.0, s1), axis=-1, keepdims=True)
        even = lax.rsqrt(even * (1.0 / channels) + 1e-06)
        odd = lax.rsqrt(odd * (1.0 / channels) + 1e-06)
        out = []
        for i, (v, inverse) in enumerate(((v0, even), (v1, jnp.where(low, even, odd)), (v2, odd))):
            scaled = v * inverse * scale[:, i * LANES : (i + 1) * LANES]
            out.append(scaled * jax.nn.sigmoid(scaled))
        return out

    def conv(plane, w, frame_at, nf, row_index, nr, taps):
        chains = [None, None]
        size = nf * nr * pairs
        done = 0
        zero = jnp.zeros((half, channels), BF16)

        def tile(a, b, i, n):
            both_columns = []
            for c in range(2):
                at = (5 * c + i) * LANES
                value = plane[
                    frame_at + a : frame_at + a + nf,
                    row_index + b : row_index + b + nr,
                    :,
                    at : at + n * LANES,
                ]
                both_columns.append(value.reshape(size, n * LANES))
            return jnp.concatenate(both_columns, axis=0)

        for a in taps:
            terms = []
            for b in range(3):
                for n in range(2):
                    terms.append(
                        (tile(a, b, 2 * n, 2), w[a, b, 2 * n * LANES : 2 * (n + 1) * LANES])
                    )
            ends = [w[a, b, 4 * LANES :] for b in range(3)] + [zero]
            terms.append(
                (
                    jnp.concatenate([tile(a, 0, 4, 1), tile(a, 2, 4, 1)], axis=-1),
                    jnp.concatenate(ends, axis=0),
                )
            )
            for lhs, rhs in terms:
                term = jnp.dot(lhs, rhs, preferred_element_type=F32)
                n = done % 2
                chains[n] = term if chains[n] is None else chains[n] + term
                done += 1
        a, b = [jnp.concatenate([c[:size], c[size:]], axis=-1) for c in chains]
        return a + b

    def piece(value, n):
        return value[n * pairs : (n + 1) * pairs]

    def put_rows(source, rows_in, target, frame_at, row_list):
        spread(source, rows_in, target)
        scale = scale_of(gain1, frame_at)
        for row, row_index in row_list:
            put(p1, norm(row_at(target, row, rows_in), scale), frame_at, row_index)

    def hidden(frame_at, nf, row, nr, saved=None):
        summed = conv(p1, w1, frame_at, nf, row - 1 + base1, nr, (0, 1, 2)) + bias1
        rounded = summed.astype(BF16).astype(F32)
        for f in range(nf):
            scale = scale_of(gain2, frame_at + f + 2)
            for r in range(nr):
                at = row + r
                inside = scale
                if sides == 2 and (at < 0 or at >= rows):
                    inside = scale * jnp.where(slot_cond[0 if at < 0 else 1], 1.0, 0.0)
                tiles = norm(piece(rounded, f * nr + r), inside)
                put(p2, tiles, frame_at + f + 2, at + 1)
                if saved is not None:
                    for i, v in enumerate(tiles):
                        saved[f, r, :, i * LANES : (i + 1) * LANES] = v.astype(BF16)

    def settle(f, values):
        valid = jnp.where(first + f < count, 1.0, 0.0)
        for r in range(rows):
            start = natural(r, rows) * pairs
            if not isinstance(start, int):
                start = pl.multiple_of(start, pairs)
            for i, v in enumerate(tiles_of(values[r] * valid)):
                own[f, i, pl.ds(start, pairs), :] = v
        for p in range(pairs):
            for i in range(3):
                value = own.at[f, i][pl.ds(p, rows, stride=pairs), :]
                at = p * flat + i * LANES
                out_ref[f, :, at : at + LANES] = value.astype(BF16)

    def with_input(f, summed):
        return [piece(summed, r) + row_at(own.at[f], r, rows) for r in range(rows)]

    count = counts_ref[0]
    for copy in small:
        copy.wait()
    gain1, bias1, gain2, bias2 = [wide(i) for i in range(4)]
    hidden_copies = []
    if sides == 1:
        parts = [(0, rows - 1), (rows - 1, 2)]
    else:
        parts = [(first_hidden, hrows)]
    for n in range(len(parts)):
        hidden_copies.append(remote(hidden_out[n], hidden_in[n], 5 + n, {"tm": tm + 1}))

    def alone():
        for f in range(frames):
            put_rows(x_ref.at[f], rows, own.at[f], f + 2, [(r, r + base1) for r in range(rows)])
        for copy in loads[0]:
            copy.wait()
        if sides == 1:
            hidden(frames - 2, 2, *parts[0], hidden_out[0])

    pl.semaphore_wait(barrier, total)
    for copy, cond in sends:
        when(cond, copy.start)
    alone()
    if sides == 1:
        when(has_next, hidden_copies[0].start)

    def halo_rows(slot):
        if sides == 1:
            return [(0, rows + base1), (1, rows + 1 + base1)]
        at = 0 if slot == 0 else rows + 2
        return [(0, at), (1, at + 1)]

    if sides == 1:
        pl.when(jnp.logical_not(has_prev))(lambda: hidden(0, frames - 2, *parts[0]))
    for slot in range(sides):
        landed = remote(
            x_ref.at[:, pl.ds(0, 2)], from_space.at[slot], slot, {"space": band}
        )
        when(slot_cond[slot], landed.wait_recv)
        for f in range(frames):
            put_rows(from_space.at[slot, f], 2, halo.at[slot, f], f + 2, halo_rows(slot))
    hidden(frames - 2, 2, *parts[-1], hidden_out[-1])
    when(has_next, hidden_copies[-1].start)

    def from_before():
        time_copy.wait_recv()
        for f in range(2):
            put_rows(from_time.at[f], rows, tail.at[f], f, [(r, r + base1) for r in range(rows)])
        for slot in range(sides):
            landed = remote(
                x_ref.at[last, pl.ds(0, 2)], from_corner.at[slot], 2 + slot, {"space": band}
            )
            when(slot_cond[slot], landed.wait_recv)
            for f in range(2):
                put_rows(from_corner.at[slot, f], 2, corner.at[slot, f], f, halo_rows(slot))
        hidden(0, frames - 2, first_hidden, hrows)

    pl.when(has_prev)(from_before)
    pl.when(jnp.logical_not(has_prev))(lambda: hidden(0, frames - 2, *parts[-1]))
    for copy in loads[1]:
        copy.wait()
    summed = conv(p2, w2, frames - 2, 2, 0, rows, (0, 1, 2)) + bias2
    for f in range(2):
        settle(
            frames - 2 + f,
            with_input(frames - 2 + f, summed[f * rows * pairs : (f + 1) * rows * pairs]),
        )
    shared = conv(p2, w2, 0, 2, 0, rows, (2,)) + bias2
    single = conv(p2, w2, 1, 1, 0, rows, (1,))
    for f in range(2):
        value = shared[f * rows * pairs : (f + 1) * rows * pairs]
        values = with_input(f, value + single if f == 1 else value)
        for r in range(rows):
            early[f, r] = values[r]

    def add_before():
        for (row, nr), ref, copy in zip(parts, hidden_in, hidden_copies):
            copy.wait_recv()
            for f in range(2):
                for r in range(nr):
                    put(p2, tiles_of(ref[f, r].astype(F32)), f, row + r + 1)
        shared = conv(p2, w2, 0, 2, 0, rows, (0,))
        single = conv(p2, w2, 0, 1, 0, rows, (1,))
        for f in range(2):
            value = shared[f * rows * pairs : (f + 1) * rows * pairs]
            summed = value + single if f == 0 else value
            settle(f, [piece(summed, r) + early[f, r] for r in range(rows)])

    def without_before():
        for f in range(2):
            settle(f, [early[f, r] for r in range(rows)])

    pl.when(has_prev)(add_before)
    pl.when(jnp.logical_not(has_prev))(without_before)
    for copy, cond in sends + [(c, has_next) for c in hidden_copies]:
        when(cond, copy.wait_send)


def shards(
    bands,
    blocks,
    latents,
    frame_counts,
    gain_first,
    bias_first,
    weight_first,
    gain_second,
    bias_second,
    weight_second,
):
    channels = gain_first.shape[0]
    frames, rows, width = latents.shape[1:]
    flat = 2 * channels
    pairs = width // flat
    x = latents.reshape(frames, rows, width)
    sides = 1 if bands == 2 else 2
    vmem = pl.BlockSpec(memory_space=pltpu.VMEM)
    hbm = pl.BlockSpec(memory_space=pltpu.HBM)
    parts = [rows - 1, 2] if sides == 1 else [rows + 2]
    scratch = pltpu.VMEM
    taps = (3, 3, 3 * channels, channels)
    rows1 = rows + (3 if sides == 1 else 4)
    out = pl.pallas_call(
        functools.partial(kernel, bands, blocks),
        out_shape=pltpu.VMEM(x.shape, BF16),
        in_specs=[pl.BlockSpec(memory_space=pltpu.SMEM)] + [hbm] * 7,
        out_specs=vmem,
        scratch_shapes=[
            scratch((4, 1, channels), F32),
            scratch((3, 3, 3 * channels, channels), BF16),
            scratch((3, 3, 3 * channels, channels), BF16),
            scratch(x.shape, BF16),
            scratch((frames + 2, rows1, pairs, 10 * LANES), BF16),
            scratch((frames + 2, rows + 2, pairs, 10 * LANES), BF16),
            scratch((frames, 3, rows * pairs, LANES), F32),
            scratch((sides, frames, 3, 2 * pairs, LANES), F32),
            scratch((2, 3, rows * pairs, LANES), F32),
            scratch((sides, 2, 3, 2 * pairs, LANES), F32),
            scratch((2, rows, pairs, flat), F32),
            scratch((2, rows, width), BF16),
            scratch((sides, frames, 2, width), BF16),
            scratch((sides, 2, 2, width), BF16),
            [scratch((2, n, pairs, flat), BF16) for n in parts],
            [scratch((2, n, pairs, flat), BF16) for n in parts],
            pltpu.SemaphoreType.DMA((11,)),
            pltpu.SemaphoreType.DMA((7,)),
            pltpu.SemaphoreType.DMA((7,)),
        ],
        compiler_params=pltpu.CompilerParams(
            collective_id=0, has_side_effects=True, vmem_limit_bytes=40 * 1024 * 1024
        ),
    )(
        frame_counts,
        pltpu.with_memory_space_constraint(x, pltpu.HBM),
        pltpu.with_memory_space_constraint(gain_first.reshape(1, channels), pltpu.HBM),
        pltpu.with_memory_space_constraint(bias_first.reshape(1, channels), pltpu.HBM),
        pltpu.with_memory_space_constraint(gain_second.reshape(1, channels), pltpu.HBM),
        pltpu.with_memory_space_constraint(bias_second.reshape(1, channels), pltpu.HBM),
        pltpu.with_memory_space_constraint(weight_first.reshape(taps), pltpu.HBM),
        pltpu.with_memory_space_constraint(weight_second.reshape(taps), pltpu.HBM),
    )
    return out.reshape(latents.shape)


def solution(mesh):
    return jax.shard_map(
        functools.partial(shards, mesh.shape["space"], mesh.shape["tm"]),
        mesh=mesh,
        in_specs=(P(("groups", "clip"), "tm", "space", None), P(("groups", "clip"))) + (P(),) * 6,
        out_specs=P(("groups", "clip"), "tm", "space", None),
        check_vma=False,
    )
```

```python
import functools

import jax
import jax.numpy as jnp
from jax import lax
from jax.experimental import pallas as pl
from jax.experimental.pallas import tpu as pltpu
from jax.sharding import PartitionSpec as P

MESH = pl.DeviceIdType.MESH
LANES = 128
BF16 = jnp.bfloat16
F32 = jnp.float32


def kernel(
    bands,
    blocks,
    counts_ref,
    x_hbm,
    gain1_hbm,
    bias1_hbm,
    gain2_hbm,
    bias2_hbm,
    w1_hbm,
    w2_hbm,
    out_ref,
    vectors,
    w1,
    w2,
    x_ref,
    p1,
    p2,
    own,
    halo,
    tail,
    corner,
    early,
    from_time,
    from_space,
    from_corner,
    hidden_out,
    hidden_in,
    l_sems,
    send_sems,
    recv_sems,
):
    frames, rows, width = x_ref.shape
    channels = vectors.shape[-1]
    flat = 2 * channels
    pairs = width // flat
    half = flat // 2 - LANES
    sides = 1 if bands == 2 else 2
    first_hidden = 0 if sides == 1 else -1
    hrows = rows + sides
    base1 = 1 if sides == 1 else 2
    tm = lax.axis_index("tm")
    band = lax.axis_index("space")
    has_prev = tm > 0
    has_next = tm < blocks - 1

    def both(a, b):
        return b if a is None else (a if b is None else jnp.logical_and(a, b))

    def when(cond, fn):
        if cond is None:
            fn()
        else:
            pl.when(cond)(fn)

    if sides == 1:
        flip = band
        links = [(1 - band, None, (1 - band) * (rows - 2), 0)]
        slot_cond = [None]
    else:
        flip = 0
        links = [
            (band - 1, band > 0, 0, 1),
            (band + 1, band < bands - 1, rows - 2, 0),
        ]
        slot_cond = [band > 0, band < bands - 1]

    peers = [({"space": p}, c) for p, c, _, _ in links]
    for step, has in ((1, has_next), (-1, has_prev)):
        peers.append(({"tm": tm + step}, has))
        peers += [({"tm": tm + step, "space": p}, both(c, has)) for p, c, _, _ in links]

    barrier = pltpu.get_barrier_semaphore()
    total = 0
    for device, cond in peers:
        when(
            cond,
            lambda device=device: pl.semaphore_signal(
                barrier, inc=1, device_id=device, device_id_type=MESH
            ),
        )
        total = total + (1 if cond is None else cond.astype(jnp.int32))

    load_x = pltpu.make_async_copy(x_hbm, x_ref, l_sems.at[0])
    loads = []
    for n, (source, target) in enumerate(((w1_hbm, w1), (w2_hbm, w2))):
        loads.append(
            [
                pltpu.make_async_copy(
                    source.at[:, b + flip * (2 - 2 * b)], target.at[:, b], l_sems.at[1 + 3 * n + b]
                )
                for b in range(3)
            ]
        )
    small = [
        pltpu.make_async_copy(source, vectors.at[i], l_sems.at[7 + i])
        for i, source in enumerate((gain1_hbm, bias1_hbm, gain2_hbm, bias2_hbm))
    ]
    load_x.start()
    for copy in small:
        copy.start()
    for copy in loads[0] + loads[1]:
        copy.start()

    def fill(ref):
        ref[...] = jnp.zeros(ref.shape, ref.dtype)

    if sides == 1:
        pad = jnp.zeros((frames + 2, 1) + p1.shape[2:], BF16)
        p1[:, 0:1] = pad
        p2[:, 0:1] = pad
    for plane in (p1, p2):
        for i in (4, 9):
            top = plane.shape[1] - 1
            plane[:, top : top + 1, :, i * LANES : (i + 1) * LANES] = jnp.zeros(
                (frames + 2, 1, pairs, LANES), BF16
            )

    def no_prev():
        p1[0:2] = jnp.zeros((2,) + p1.shape[1:], BF16)

    pl.when(jnp.logical_not(has_prev))(no_prev)
    if sides == 2:
        for slot in range(2):

            def outside(slot=slot):
                from_space[slot] = jnp.zeros(from_space.shape[1:], BF16)

            def outside_corner(slot=slot):
                from_corner[slot] = jnp.zeros(from_corner.shape[1:], BF16)

            pl.when(jnp.logical_not(slot_cond[slot]))(outside)
            pl.when(jnp.logical_and(jnp.logical_not(slot_cond[slot]), has_prev))(outside_corner)

    load_x.wait()

    def remote(src, dst, at, device):
        return pltpu.make_async_remote_copy(
            src_ref=src,
            dst_ref=dst,
            send_sem=send_sems.at[at],
            recv_sem=recv_sems.at[at],
            device_id=device,
            device_id_type=MESH,
        )

    last = pl.ds(frames - 2, 2)
    sends = []
    for peer, cond, edge, slot in links:
        copy = remote(x_ref.at[:, pl.ds(edge, 2)], from_space.at[slot], slot, {"space": peer})
        sends.append((copy, cond))
    time_copy = remote(x_ref.at[last], from_time, 4, {"tm": tm + 1})
    sends.append((time_copy, has_next))
    for peer, cond, edge, slot in links:
        copy = remote(
            x_ref.at[last, pl.ds(edge, 2)],
            from_corner.at[slot],
            2 + slot,
            {"tm": tm + 1, "space": peer},
        )
        sends.append((copy, both(cond, has_next)))

    first = tm * frames
    lane = lax.broadcasted_iota(jnp.int32, (pairs, LANES), 1)
    pair = lax.broadcasted_iota(jnp.int32, (pairs, LANES), 0)
    low = lane < half

    def wide(i):
        value = vectors[i]
        return jnp.concatenate([value, value], axis=-1)

    def scale_of(gain, frame_at):
        return gain * jnp.where(first - 2 + frame_at < count, 1.0, 0.0)

    def natural(row, size):
        if sides == 2:
            return row
        return row + flip * (size - 1 - 2 * row)

    def spread(source, rows_in, target):
        for p in range(pairs):
            for i in range(3):
                at = p * flat + i * LANES
                part = source[:, at : at + LANES].astype(F32)
                target.at[i][pl.ds(p, rows_in, stride=pairs), :] = part

    def row_at(ref, row, size):
        start = natural(row, size) * pairs
        if not isinstance(start, int):
            start = pl.multiple_of(start, pairs)
        return jnp.concatenate([ref[i, pl.ds(start, pairs), :] for i in range(3)], axis=-1)

    def before(v):
        return jnp.where(pair > 0, pltpu.roll(v, 1, 0), 0.0)

    def after(v):
        return jnp.where(pair < pairs - 1, pltpu.roll(v, pairs - 1, 0), 0.0)

    def put(plane, tiles, frame_at, row_index):
        v0, v1, v2 = tiles
        r0, r1, r2 = [pltpu.roll(v, half, 1) for v in tiles]
        joint = jnp.where(low, r1, r2)
        nearby = after(v1)
        even = (before(joint), jnp.where(low, before(r2), r0), jnp.where(low, r0, r1), joint)
        odd = (v0, v1, v2, after(v0))
        for n, (values, end, raised) in enumerate(
            ((even, r2, v2), (odd, nearby, pltpu.roll(nearby, half, 1)))
        ):
            at = 5 * n * LANES
            for i, v in enumerate(values):
                plane[frame_at, row_index, :, at + i * LANES : at + (i + 1) * LANES] = v.astype(BF16)
            at += 4 * LANES
            plane[frame_at, row_index, :, at : at + half] = end[:, :half].astype(BF16)
            if row_index > 0:
                plane[frame_at, row_index - 1, :, at + half : at + LANES] = raised[:, half:].astype(
                    BF16
                )

    def tiles_of(value):
        return [value[:, i * LANES : (i + 1) * LANES] for i in range(3)]

    def norm(value, scale):
        v0, v1, v2 = tiles_of(value)
        s1 = v1 * v1
        even = jnp.sum(v0 * v0 + jnp.where(low, s1, 0.0), axis=-1, keepdims=True)
        odd = jnp.sum(v2 * v2 + jnp.where(low, 0.0, s1), axis=-1, keepdims=True)
        even = lax.rsqrt(even * (1.0 / channels) + 1e-06)
        odd = lax.rsqrt(odd * (1.0 / channels) + 1e-06)
        out = []
        for i, (v, inverse) in enumerate(((v0, even), (v1, jnp.where(low, even, odd)), (v2, odd))):
            scaled = v * inverse * scale[:, i * LANES : (i + 1) * LANES]
            out.append(scaled * jax.nn.sigmoid(scaled))
        return out

    def conv(plane, w, frame_at, nf, row_index, nr, taps):
        chains = [None, None]
        size = nf * nr * pairs
        done = 0
        zero = jnp.zeros((half, channels), BF16)

        def tile(a, b, i, n):
            both_columns = []
            for c in range(2):
                at = (5 * c + i) * LANES
                value = plane[
                    frame_at + a : frame_at + a + nf,
                    row_index + b : row_index + b + nr,
                    :,
                    at : at + n * LANES,
                ]
                both_columns.append(value.reshape(size, n * LANES))
            return jnp.concatenate(both_columns, axis=0)

        for a in taps:
            terms = []
            for b in range(3):
                for n in range(2):
                    terms.append(
                        (tile(a, b, 2 * n, 2), w[a, b, 2 * n * LANES : 2 * (n + 1) * LANES])
                    )
            ends = [w[a, b, 4 * LANES :] for b in range(3)] + [zero]
            terms.append(
                (
                    jnp.concatenate([tile(a, 0, 4, 1), tile(a, 2, 4, 1)], axis=-1),
                    jnp.concatenate(ends, axis=0),
                )
            )
            for lhs, rhs in terms:
                term = jnp.dot(lhs, rhs, preferred_element_type=F32)
                n = done % 2
                chains[n] = term if chains[n] is None else chains[n] + term
                done += 1
        a, b = [jnp.concatenate([c[:size], c[size:]], axis=-1) for c in chains]
        return a + b

    def piece(value, n):
        return value[n * pairs : (n + 1) * pairs]

    def put_rows(source, rows_in, target, frame_at, row_list):
        spread(source, rows_in, target)
        scale = scale_of(gain1, frame_at)
        for row, row_index in row_list:
            put(p1, norm(row_at(target, row, rows_in), scale), frame_at, row_index)

    def hidden(frame_at, nf, row, nr, saved=None):
        summed = conv(p1, w1, frame_at, nf, row - 1 + base1, nr, (0, 1, 2)) + bias1
        rounded = summed.astype(BF16).astype(F32)
        for f in range(nf):
            scale = scale_of(gain2, frame_at + f + 2)
            for r in range(nr):
                at = row + r
                inside = scale
                if sides == 2 and (at < 0 or at >= rows):
                    inside = scale * jnp.where(slot_cond[0 if at < 0 else 1], 1.0, 0.0)
                tiles = norm(piece(rounded, f * nr + r), inside)
                put(p2, tiles, frame_at + f + 2, at + 1)
                if saved is not None:
                    for i, v in enumerate(tiles):
                        saved[f, r, :, i * LANES : (i + 1) * LANES] = v.astype(BF16)

    def settle(f, values):
        valid = jnp.where(first + f < count, 1.0, 0.0)
        for r in range(rows):
            start = natural(r, rows) * pairs
            if not isinstance(start, int):
                start = pl.multiple_of(start, pairs)
            for i, v in enumerate(tiles_of(values[r] * valid)):
                own[f, i, pl.ds(start, pairs), :] = v
        for p in range(pairs):
            for i in range(3):
                value = own.at[f, i][pl.ds(p, rows, stride=pairs), :]
                at = p * flat + i * LANES
                out_ref[f, :, at : at + LANES] = value.astype(BF16)

    def with_input(f, summed):
        return [piece(summed, r) + row_at(own.at[f], r, rows) for r in range(rows)]

    count = counts_ref[0]
    for copy in small:
        copy.wait()
    gain1, bias1, gain2, bias2 = [wide(i) for i in range(4)]
    hidden_copies = []
    if sides == 1:
        parts = [(0, rows - 1), (rows - 1, 2)]
    else:
        parts = [(first_hidden, hrows)]
    for n in range(len(parts)):
        hidden_copies.append(remote(hidden_out[n], hidden_in[n], 5 + n, {"tm": tm + 1}))

    pl.semaphore_wait(barrier, total)
    for copy, cond in sends:
        when(cond, copy.start)
    for copy in loads[0]:
        copy.wait()
    for f in range(frames):
        put_rows(x_ref.at[f], rows, own.at[f], f + 2, [(r, r + base1) for r in range(rows)])
    if sides == 1:
        hidden(frames - 2, 2, *parts[0], hidden_out[0])
        when(has_next, hidden_copies[0].start)

    def halo_rows(slot):
        if sides == 1:
            return [(0, rows + base1), (1, rows + 1 + base1)]
        at = 0 if slot == 0 else rows + 2
        return [(0, at), (1, at + 1)]

    if sides == 1:
        pl.when(jnp.logical_not(has_prev))(lambda: hidden(0, frames - 2, *parts[0]))
    for slot in range(sides):
        landed = remote(
            x_ref.at[:, pl.ds(0, 2)], from_space.at[slot], slot, {"space": band}
        )
        when(slot_cond[slot], landed.wait_recv)
        for f in range(frames):
            put_rows(from_space.at[slot, f], 2, halo.at[slot, f], f + 2, halo_rows(slot))
    hidden(frames - 2, 2, *parts[-1], hidden_out[-1])
    when(has_next, hidden_copies[-1].start)

    def finish():
        for f in range(frames - 2, frames):
            settle(f, with_input(f, conv(p2, w2, f, 1, 0, rows, (0, 1, 2)) + bias2))

    def start_first():
        shared = conv(p2, w2, 0, 2, 0, rows, (2,)) + bias2
        single = conv(p2, w2, 1, 1, 0, rows, (1,))
        values = []
        for f in range(2):
            value = shared[f * rows * pairs : (f + 1) * rows * pairs]
            values.append(with_input(f, value + single if f == 1 else value))
        return values

    def fetch(n):
        (row, nr), ref = parts[n], hidden_in[n]
        hidden_copies[n].wait_recv()
        for f in range(2):
            for r in range(nr):
                put(p2, tiles_of(ref[f, r].astype(F32)), f, row + r + 1)

    def from_before():
        time_copy.wait_recv()
        for slot in range(sides):
            landed = remote(
                x_ref.at[last, pl.ds(0, 2)], from_corner.at[slot], 2 + slot, {"space": band}
            )
            when(slot_cond[slot], landed.wait_recv)
        for f in range(2):
            put_rows(from_time.at[f], rows, tail.at[f], f, [(r, r + base1) for r in range(rows)])
            for slot in range(sides):
                put_rows(from_corner.at[slot, f], 2, corner.at[slot, f], f, halo_rows(slot))
        for f in range(frames - 2):
            hidden(f, 1, first_hidden, hrows)
        if sides == 1:
            fetch(0)
        finish()
        values = start_first()
        for f in range(2):
            for r in range(rows):
                early[f, r] = values[f][r]
        fetch(len(parts) - 1)
        shared = conv(p2, w2, 0, 2, 0, rows, (0,))
        single = conv(p2, w2, 0, 1, 0, rows, (1,))
        for f in range(2):
            value = shared[f * rows * pairs : (f + 1) * rows * pairs]
            summed = value + single if f == 0 else value
            settle(f, [piece(summed, r) + early[f, r] for r in range(rows)])

    def without_before():
        hidden(0, frames - 2, *parts[-1])
        finish()
        values = start_first()
        for f in range(2):
            settle(f, values[f])

    for copy in loads[1]:
        copy.wait()
    pl.when(has_prev)(from_before)
    pl.when(jnp.logical_not(has_prev))(without_before)
    for copy, cond in sends + [(c, has_next) for c in hidden_copies]:
        when(cond, copy.wait_send)


def shards(
    bands,
    blocks,
    latents,
    frame_counts,
    gain_first,
    bias_first,
    weight_first,
    gain_second,
    bias_second,
    weight_second,
):
    channels = gain_first.shape[0]
    frames, rows, width = latents.shape[1:]
    flat = 2 * channels
    pairs = width // flat
    x = latents.reshape(frames, rows, width)
    sides = 1 if bands == 2 else 2
    vmem = pl.BlockSpec(memory_space=pltpu.VMEM)
    hbm = pl.BlockSpec(memory_space=pltpu.HBM)
    parts = [rows - 1, 2] if sides == 1 else [rows + 2]
    scratch = pltpu.VMEM
    taps = (3, 3, 3 * channels, channels)
    rows1 = rows + (3 if sides == 1 else 4)
    out = pl.pallas_call(
        functools.partial(kernel, bands, blocks),
        out_shape=pltpu.VMEM(x.shape, BF16),
        in_specs=[pl.BlockSpec(memory_space=pltpu.SMEM)] + [hbm] * 7,
        out_specs=vmem,
        scratch_shapes=[
            scratch((4, 1, channels), F32),
            scratch((3, 3, 3 * channels, channels), BF16),
            scratch((3, 3, 3 * channels, channels), BF16),
            scratch(x.shape, BF16),
            scratch((frames + 2, rows1, pairs, 10 * LANES), BF16),
            scratch((frames + 2, rows + 2, pairs, 10 * LANES), BF16),
            scratch((frames, 3, rows * pairs, LANES), F32),
            scratch((sides, frames, 3, 2 * pairs, LANES), F32),
            scratch((2, 3, rows * pairs, LANES), F32),
            scratch((sides, 2, 3, 2 * pairs, LANES), F32),
            scratch((2, rows, pairs, flat), F32),
            scratch((2, rows, width), BF16),
            scratch((sides, frames, 2, width), BF16),
            scratch((sides, 2, 2, width), BF16),
            [scratch((2, n, pairs, flat), BF16) for n in parts],
            [scratch((2, n, pairs, flat), BF16) for n in parts],
            pltpu.SemaphoreType.DMA((11,)),
            pltpu.SemaphoreType.DMA((7,)),
            pltpu.SemaphoreType.DMA((7,)),
        ],
        compiler_params=pltpu.CompilerParams(
            collective_id=0, has_side_effects=True, vmem_limit_bytes=40 * 1024 * 1024
        ),
    )(
        frame_counts,
        pltpu.with_memory_space_constraint(x, pltpu.HBM),
        pltpu.with_memory_space_constraint(gain_first.reshape(1, channels), pltpu.HBM),
        pltpu.with_memory_space_constraint(bias_first.reshape(1, channels), pltpu.HBM),
        pltpu.with_memory_space_constraint(gain_second.reshape(1, channels), pltpu.HBM),
        pltpu.with_memory_space_constraint(bias_second.reshape(1, channels), pltpu.HBM),
        pltpu.with_memory_space_constraint(weight_first.reshape(taps), pltpu.HBM),
        pltpu.with_memory_space_constraint(weight_second.reshape(taps), pltpu.HBM),
    )
    return out.reshape(latents.shape)


def solution(mesh):
    return jax.shard_map(
        functools.partial(shards, mesh.shape["space"], mesh.shape["tm"]),
        mesh=mesh,
        in_specs=(P(("groups", "clip"), "tm", "space", None), P(("groups", "clip"))) + (P(),) * 6,
        out_specs=P(("groups", "clip"), "tm", "space", None),
        check_vma=False,
    )
```

```python
import functools

import jax
import jax.numpy as jnp
from jax import lax
from jax.experimental import pallas as pl
from jax.experimental.pallas import tpu as pltpu
from jax.sharding import PartitionSpec as P

MESH = pl.DeviceIdType.MESH
LANES = 128
BF16 = jnp.bfloat16
F32 = jnp.float32


def kernel(
    bands,
    blocks,
    counts_ref,
    x_hbm,
    gain1_hbm,
    bias1_hbm,
    gain2_hbm,
    bias2_hbm,
    w1_hbm,
    w2_hbm,
    out_ref,
    vectors,
    w1,
    w2,
    x_ref,
    p1,
    p2,
    own,
    halo,
    tail,
    corner,
    early,
    begun,
    from_time,
    from_space,
    from_corner,
    hidden_out,
    hidden_in,
    l_sems,
    send_sems,
    recv_sems,
):
    frames, rows, width = x_ref.shape
    channels = vectors.shape[-1]
    flat = 2 * channels
    pairs = width // flat
    half = flat // 2 - LANES
    sides = 1 if bands == 2 else 2
    first_hidden = 0 if sides == 1 else -1
    hrows = rows + sides
    base1 = 1 if sides == 1 else 2
    tm = lax.axis_index("tm")
    band = lax.axis_index("space")
    has_prev = tm > 0
    has_next = tm < blocks - 1

    def both(a, b):
        return b if a is None else (a if b is None else jnp.logical_and(a, b))

    def when(cond, fn):
        if cond is None:
            fn()
        else:
            pl.when(cond)(fn)

    if sides == 1:
        flip = band
        links = [(1 - band, None, (1 - band) * (rows - 2), 0)]
        slot_cond = [None]
    else:
        flip = 0
        links = [
            (band - 1, band > 0, 0, 1),
            (band + 1, band < bands - 1, rows - 2, 0),
        ]
        slot_cond = [band > 0, band < bands - 1]

    peers = [({"space": p}, c) for p, c, _, _ in links]
    for step, has in ((1, has_next), (-1, has_prev)):
        peers.append(({"tm": tm + step}, has))
        peers += [({"tm": tm + step, "space": p}, both(c, has)) for p, c, _, _ in links]

    barrier = pltpu.get_barrier_semaphore()
    total = 0
    for device, cond in peers:
        when(
            cond,
            lambda device=device: pl.semaphore_signal(
                barrier, inc=1, device_id=device, device_id_type=MESH
            ),
        )
        total = total + (1 if cond is None else cond.astype(jnp.int32))

    load_x = pltpu.make_async_copy(x_hbm, x_ref, l_sems.at[0])
    loads = []
    for n, (source, target) in enumerate(((w1_hbm, w1), (w2_hbm, w2))):
        loads.append(
            [
                pltpu.make_async_copy(
                    source.at[:, b + flip * (2 - 2 * b)], target.at[:, b], l_sems.at[1 + 3 * n + b]
                )
                for b in range(3)
            ]
        )
    small = [
        pltpu.make_async_copy(source, vectors.at[i], l_sems.at[7 + i])
        for i, source in enumerate((gain1_hbm, bias1_hbm, gain2_hbm, bias2_hbm))
    ]
    load_x.start()
    for copy in small:
        copy.start()
    for copy in loads[0] + loads[1]:
        copy.start()

    def fill(ref):
        ref[...] = jnp.zeros(ref.shape, ref.dtype)

    if sides == 1:
        pad = jnp.zeros((frames + 2, 1) + p1.shape[2:], BF16)
        p1[:, 0:1] = pad
        p2[:, 0:1] = pad
    for plane in (p1, p2):
        for i in (4, 9):
            top = plane.shape[1] - 1
            plane[:, top : top + 1, :, i * LANES : (i + 1) * LANES] = jnp.zeros(
                (frames + 2, 1, pairs, LANES), BF16
            )

    def no_prev():
        p1[0:2] = jnp.zeros((2,) + p1.shape[1:], BF16)

    pl.when(jnp.logical_not(has_prev))(no_prev)
    if sides == 2:
        for slot in range(2):

            def outside(slot=slot):
                from_space[slot] = jnp.zeros(from_space.shape[1:], BF16)

            def outside_corner(slot=slot):
                from_corner[slot] = jnp.zeros(from_corner.shape[1:], BF16)

            pl.when(jnp.logical_not(slot_cond[slot]))(outside)
            pl.when(jnp.logical_and(jnp.logical_not(slot_cond[slot]), has_prev))(outside_corner)

    load_x.wait()

    def remote(src, dst, at, device):
        return pltpu.make_async_remote_copy(
            src_ref=src,
            dst_ref=dst,
            send_sem=send_sems.at[at],
            recv_sem=recv_sems.at[at],
            device_id=device,
            device_id_type=MESH,
        )

    last = pl.ds(frames - 2, 2)
    sends = []
    for peer, cond, edge, slot in links:
        copy = remote(x_ref.at[:, pl.ds(edge, 2)], from_space.at[slot], slot, {"space": peer})
        sends.append((copy, cond))
    time_copy = remote(x_ref.at[last], from_time, 4, {"tm": tm + 1})
    sends.append((time_copy, has_next))
    for peer, cond, edge, slot in links:
        copy = remote(
            x_ref.at[last, pl.ds(edge, 2)],
            from_corner.at[slot],
            2 + slot,
            {"tm": tm + 1, "space": peer},
        )
        sends.append((copy, both(cond, has_next)))

    first = tm * frames
    lane = lax.broadcasted_iota(jnp.int32, (pairs, LANES), 1)
    pair = lax.broadcasted_iota(jnp.int32, (pairs, LANES), 0)
    low = lane < half

    def wide(i):
        value = vectors[i]
        return jnp.concatenate([value, value], axis=-1)

    def scale_of(gain, frame_at):
        return gain * jnp.where(first - 2 + frame_at < count, 1.0, 0.0)

    def natural(row, size):
        if sides == 2:
            return row
        return row + flip * (size - 1 - 2 * row)

    def spread(source, rows_in, target):
        for p in range(pairs):
            for i in range(3):
                at = p * flat + i * LANES
                part = source[:, at : at + LANES].astype(F32)
                target.at[i][pl.ds(p, rows_in, stride=pairs), :] = part

    def row_at(ref, row, size):
        start = natural(row, size) * pairs
        if not isinstance(start, int):
            start = pl.multiple_of(start, pairs)
        return jnp.concatenate([ref[i, pl.ds(start, pairs), :] for i in range(3)], axis=-1)

    def before(v):
        return jnp.where(pair > 0, pltpu.roll(v, 1, 0), 0.0)

    def after(v):
        return jnp.where(pair < pairs - 1, pltpu.roll(v, pairs - 1, 0), 0.0)

    def put(plane, tiles, frame_at, row_index):
        v0, v1, v2 = tiles
        r0, r1, r2 = [pltpu.roll(v, half, 1) for v in tiles]
        joint = jnp.where(low, r1, r2)
        nearby = after(v1)
        even = (before(joint), jnp.where(low, before(r2), r0), jnp.where(low, r0, r1), joint)
        odd = (v0, v1, v2, after(v0))
        for n, (values, end, raised) in enumerate(
            ((even, r2, v2), (odd, nearby, pltpu.roll(nearby, half, 1)))
        ):
            at = 5 * n * LANES
            for i, v in enumerate(values):
                plane[frame_at, row_index, :, at + i * LANES : at + (i + 1) * LANES] = v.astype(BF16)
            at += 4 * LANES
            plane[frame_at, row_index, :, at : at + half] = end[:, :half].astype(BF16)
            if row_index > 0:
                plane[frame_at, row_index - 1, :, at + half : at + LANES] = raised[:, half:].astype(
                    BF16
                )

    def tiles_of(value):
        return [value[:, i * LANES : (i + 1) * LANES] for i in range(3)]

    def norm(value, scale):
        v0, v1, v2 = tiles_of(value)
        s1 = v1 * v1
        even = jnp.sum(v0 * v0 + jnp.where(low, s1, 0.0), axis=-1, keepdims=True)
        odd = jnp.sum(v2 * v2 + jnp.where(low, 0.0, s1), axis=-1, keepdims=True)
        even = lax.rsqrt(even * (1.0 / channels) + 1e-06)
        odd = lax.rsqrt(odd * (1.0 / channels) + 1e-06)
        out = []
        for i, (v, inverse) in enumerate(((v0, even), (v1, jnp.where(low, even, odd)), (v2, odd))):
            scaled = v * inverse * scale[:, i * LANES : (i + 1) * LANES]
            out.append(scaled * jax.nn.sigmoid(scaled))
        return out

    def conv(plane, w, frame_at, nf, row_index, nr, taps, across=(0, 1, 2), end=True):
        chains = [None, None]
        size = nf * nr * pairs
        done = 0
        zero = jnp.zeros((half, channels), BF16)

        def tile(a, b, i, n):
            both_columns = []
            for c in range(2):
                at = (5 * c + i) * LANES
                value = plane[
                    frame_at + a : frame_at + a + nf,
                    row_index + b : row_index + b + nr,
                    :,
                    at : at + n * LANES,
                ]
                both_columns.append(value.reshape(size, n * LANES))
            return jnp.concatenate(both_columns, axis=0)

        for a in taps:
            terms = []
            for b in across:
                for n in range(2):
                    terms.append(
                        (tile(a, b, 2 * n, 2), w[a, b, 2 * n * LANES : 2 * (n + 1) * LANES])
                    )
            if end:
                ends = [w[a, b, 4 * LANES :] for b in range(3)] + [zero]
                terms.append(
                    (
                        jnp.concatenate([tile(a, 0, 4, 1), tile(a, 2, 4, 1)], axis=-1),
                        jnp.concatenate(ends, axis=0),
                    )
                )
            for lhs, rhs in terms:
                term = jnp.dot(lhs, rhs, preferred_element_type=F32)
                n = done % 2
                chains[n] = term if chains[n] is None else chains[n] + term
                done += 1
        a, b = [jnp.concatenate([c[:size], c[size:]], axis=-1) for c in chains]
        return a + b

    def piece(value, n):
        return value[n * pairs : (n + 1) * pairs]

    def put_rows(source, rows_in, target, frame_at, row_list):
        spread(source, rows_in, target)
        scale = scale_of(gain1, frame_at)
        for row, row_index in row_list:
            put(p1, norm(row_at(target, row, rows_in), scale), frame_at, row_index)

    def beside(frame_at, nf, row):
        at = row - 1 + base1
        lower = conv(p1, w1, frame_at, nf, at, 2, (0, 1, 2), (0,), False)
        own_row = conv(p1, w1, frame_at, nf, at, 1, (0, 1, 2), (1,), False)
        for f in range(nf):
            begun[f, 0] = piece(lower, 2 * f) + piece(own_row, f)
            begun[f, 1] = piece(lower, 2 * f + 1)

    def hidden(frame_at, nf, row, nr, saved=None, rest=False):
        at = row - 1 + base1
        if rest:
            upper = conv(p1, w1, frame_at, nf, at, 2, (0, 1, 2), (2,))
            last_row = conv(p1, w1, frame_at, nf, at + 1, 1, (0, 1, 2), (1,), False)
            values = []
            for f in range(nf):
                values.append(piece(upper, 2 * f) + begun[f, 0])
                values.append(piece(upper, 2 * f + 1) + piece(last_row, f) + begun[f, 1])
            summed = jnp.concatenate(values, axis=0) + bias1
        else:
            summed = conv(p1, w1, frame_at, nf, at, nr, (0, 1, 2)) + bias1
        rounded = summed.astype(BF16).astype(F32)
        for f in range(nf):
            scale = scale_of(gain2, frame_at + f + 2)
            for r in range(nr):
                at = row + r
                inside = scale
                if sides == 2 and (at < 0 or at >= rows):
                    inside = scale * jnp.where(slot_cond[0 if at < 0 else 1], 1.0, 0.0)
                tiles = norm(piece(rounded, f * nr + r), inside)
                put(p2, tiles, frame_at + f + 2, at + 1)
                if saved is not None:
                    for i, v in enumerate(tiles):
                        saved[f, r, :, i * LANES : (i + 1) * LANES] = v.astype(BF16)

    def settle(f, values):
        valid = jnp.where(first + f < count, 1.0, 0.0)
        for r in range(rows):
            start = natural(r, rows) * pairs
            if not isinstance(start, int):
                start = pl.multiple_of(start, pairs)
            for i, v in enumerate(tiles_of(values[r] * valid)):
                own[f, i, pl.ds(start, pairs), :] = v
        for p in range(pairs):
            for i in range(3):
                value = own.at[f, i][pl.ds(p, rows, stride=pairs), :]
                at = p * flat + i * LANES
                out_ref[f, :, at : at + LANES] = value.astype(BF16)

    def with_input(f, summed):
        return [piece(summed, r) + row_at(own.at[f], r, rows) for r in range(rows)]

    count = counts_ref[0]
    for copy in small:
        copy.wait()
    gain1, bias1, gain2, bias2 = [wide(i) for i in range(4)]
    hidden_copies = []
    if sides == 1:
        parts = [(0, rows - 1), (rows - 1, 2)]
    else:
        parts = [(first_hidden, hrows)]
    for n in range(len(parts)):
        hidden_copies.append(remote(hidden_out[n], hidden_in[n], 5 + n, {"tm": tm + 1}))

    pl.semaphore_wait(barrier, total)
    for copy, cond in sends:
        when(cond, copy.start)
    for copy in loads[0]:
        copy.wait()
    for f in range(frames):
        put_rows(x_ref.at[f], rows, own.at[f], f + 2, [(r, r + base1) for r in range(rows)])
    if sides == 1:
        hidden(frames - 2, 2, *parts[0], hidden_out[0])
        when(has_next, hidden_copies[0].start)
        beside(frames - 2, 2, parts[1][0])

    def halo_rows(slot):
        if sides == 1:
            return [(0, rows + base1), (1, rows + 1 + base1)]
        at = 0 if slot == 0 else rows + 2
        return [(0, at), (1, at + 1)]

    if sides == 1:
        pl.when(jnp.logical_not(has_prev))(lambda: hidden(0, frames - 2, *parts[0]))
    for copy in loads[1]:
        copy.wait()
    for slot in range(sides):
        landed = remote(
            x_ref.at[:, pl.ds(0, 2)], from_space.at[slot], slot, {"space": band}
        )
        when(slot_cond[slot], landed.wait_recv)
        for f in range(frames):
            put_rows(from_space.at[slot, f], 2, halo.at[slot, f], f + 2, halo_rows(slot))
    hidden(frames - 2, 2, *parts[-1], None, sides == 1)
    out_row, out_rows = (rows - 2, 2) if sides == 1 else (0, rows)

    def forward():
        shared = conv(p2, w2, frames, 2, out_row, out_rows, (0,))
        single = conv(p2, w2, frames, 1, out_row, out_rows, (1,))
        for f in range(2):
            for r in range(out_rows):
                value = piece(shared, f * out_rows + r)
                value = value + piece(single, r) if f == 0 else value
                for i, v in enumerate(tiles_of(value)):
                    hidden_out[-1][f, r, :, i * LANES : (i + 1) * LANES] = v.astype(BF16)
        hidden_copies[-1].start()

    pl.when(has_next)(forward)

    def finish():
        summed = conv(p2, w2, frames - 2, 2, 0, rows, (0, 1, 2)) + bias2
        for f in range(2):
            settle(
                frames - 2 + f,
                with_input(frames - 2 + f, summed[f * rows * pairs : (f + 1) * rows * pairs]),
            )

    def start_first():
        shared = conv(p2, w2, 0, 2, 0, rows, (2,)) + bias2
        single = conv(p2, w2, 1, 1, 0, rows, (1,))
        values = []
        for f in range(2):
            value = shared[f * rows * pairs : (f + 1) * rows * pairs]
            values.append(with_input(f, value + single if f == 1 else value))
        return values

    def fetch(n):
        (row, nr), ref = parts[n], hidden_in[n]
        hidden_copies[n].wait_recv()
        for f in range(2):
            for r in range(nr):
                put(p2, tiles_of(ref[f, r].astype(F32)), f, row + r + 1)

    def from_before():
        time_copy.wait_recv()
        for slot in range(sides):
            landed = remote(
                x_ref.at[last, pl.ds(0, 2)], from_corner.at[slot], 2 + slot, {"space": band}
            )
            when(slot_cond[slot], landed.wait_recv)
        for f in range(2):
            put_rows(from_time.at[f], rows, tail.at[f], f, [(r, r + base1) for r in range(rows)])
            for slot in range(sides):
                put_rows(from_corner.at[slot, f], 2, corner.at[slot, f], f, halo_rows(slot))
        for f in range(frames - 2):
            hidden(f, 1, first_hidden, hrows)
        if sides == 1:
            fetch(0)
        finish()
        values = start_first()
        if sides == 1:
            shared = conv(p2, w2, 0, 2, 0, out_row, (0,))
            single = conv(p2, w2, 0, 1, 0, out_row, (1,))
            for r in range(out_row):
                values[0][r] = values[0][r] + piece(shared, r) + piece(single, r)
                values[1][r] = values[1][r] + piece(shared, out_row + r)
        for f in range(2):
            for r in range(rows):
                early[f, r] = values[f][r]
        hidden_copies[-1].wait_recv()
        for f in range(2):
            values = [early[f, r] for r in range(rows)]
            for r in range(out_rows):
                at = out_row + r
                values[at] = values[at] + hidden_in[-1][f, r].astype(F32)
            settle(f, values)

    def without_before():
        hidden(0, frames - 2, *parts[-1])
        finish()
        values = start_first()
        for f in range(2):
            settle(f, values[f])

    pl.when(has_prev)(from_before)
    pl.when(jnp.logical_not(has_prev))(without_before)
    for copy, cond in sends + [(c, has_next) for c in hidden_copies]:
        when(cond, copy.wait_send)


def shards(
    bands,
    blocks,
    latents,
    frame_counts,
    gain_first,
    bias_first,
    weight_first,
    gain_second,
    bias_second,
    weight_second,
):
    channels = gain_first.shape[0]
    frames, rows, width = latents.shape[1:]
    flat = 2 * channels
    pairs = width // flat
    x = latents.reshape(frames, rows, width)
    sides = 1 if bands == 2 else 2
    vmem = pl.BlockSpec(memory_space=pltpu.VMEM)
    hbm = pl.BlockSpec(memory_space=pltpu.HBM)
    parts = [rows - 1, 2] if sides == 1 else [rows]
    scratch = pltpu.VMEM
    taps = (3, 3, 3 * channels, channels)
    rows1 = rows + (3 if sides == 1 else 4)
    out = pl.pallas_call(
        functools.partial(kernel, bands, blocks),
        out_shape=pltpu.VMEM(x.shape, BF16),
        in_specs=[pl.BlockSpec(memory_space=pltpu.SMEM)] + [hbm] * 7,
        out_specs=vmem,
        scratch_shapes=[
            scratch((4, 1, channels), F32),
            scratch((3, 3, 3 * channels, channels), BF16),
            scratch((3, 3, 3 * channels, channels), BF16),
            scratch(x.shape, BF16),
            scratch((frames + 2, rows1, pairs, 10 * LANES), BF16),
            scratch((frames + 2, rows + 2, pairs, 10 * LANES), BF16),
            scratch((frames, 3, rows * pairs, LANES), F32),
            scratch((sides, frames, 3, 2 * pairs, LANES), F32),
            scratch((2, 3, rows * pairs, LANES), F32),
            scratch((sides, 2, 3, 2 * pairs, LANES), F32),
            scratch((2, rows, pairs, flat), F32),
            scratch((2, 2, pairs, flat), F32),
            scratch((2, rows, width), BF16),
            scratch((sides, frames, 2, width), BF16),
            scratch((sides, 2, 2, width), BF16),
            [scratch((2, n, pairs, flat), BF16) for n in parts],
            [scratch((2, n, pairs, flat), BF16) for n in parts],
            pltpu.SemaphoreType.DMA((11,)),
            pltpu.SemaphoreType.DMA((7,)),
            pltpu.SemaphoreType.DMA((7,)),
        ],
        compiler_params=pltpu.CompilerParams(
            collective_id=0, has_side_effects=True, vmem_limit_bytes=40 * 1024 * 1024
        ),
    )(
        frame_counts,
        pltpu.with_memory_space_constraint(x, pltpu.HBM),
        pltpu.with_memory_space_constraint(gain_first.reshape(1, channels), pltpu.HBM),
        pltpu.with_memory_space_constraint(bias_first.reshape(1, channels), pltpu.HBM),
        pltpu.with_memory_space_constraint(gain_second.reshape(1, channels), pltpu.HBM),
        pltpu.with_memory_space_constraint(bias_second.reshape(1, channels), pltpu.HBM),
        pltpu.with_memory_space_constraint(weight_first.reshape(taps), pltpu.HBM),
        pltpu.with_memory_space_constraint(weight_second.reshape(taps), pltpu.HBM),
    )
    return out.reshape(latents.shape)


def solution(mesh):
    return jax.shard_map(
        functools.partial(shards, mesh.shape["space"], mesh.shape["tm"]),
        mesh=mesh,
        in_specs=(P(("groups", "clip"), "tm", "space", None), P(("groups", "clip"))) + (P(),) * 6,
        out_specs=P(("groups", "clip"), "tm", "space", None),
        check_vma=False,
    )
```
